512 devices in a mesh: wide: 64 (over y, x, core), tall: 8 (over z).
Axes of the slice: x: 4, y: 8, z: 8, core: 2. Of those that a mesh axis runs over, the one named last changes fastest.
Arguments:
- tokens: bfloat16 [192, 1536, 512], P('tall', 'wide'), may hold values from -6 to 6
- qkv_weight: bfloat16 [512, 1536], replicated, may hold values from -0.25 to 0.25
- proj_weight: bfloat16 [512, 512], replicated, may hold values from -0.25 to 0.25
- head_scale: float32 [16], replicated, may hold values from 5 to 100
- attn_gain: float32 [512], replicated, may hold values from 0.5 to 1.5
- router: bfloat16 [512, 64], replicated, may hold values from -0.25 to 0.25
- expert_in: bfloat16 [64, 512, 2048], P('wide', None, 'tall'), may hold values from -0.25 to 0.25
- expert_out: bfloat16 [64, 2048, 512], P('wide', 'tall'), may hold values from -0.125 to 0.125
- moe_gain: float32 [512], replicated, may hold values from 0.5 to 1.5
- expert_ids: int32 [8, 64, 576, 1], P('tall', 'wide'), may hold values from 0 to 63; in each aligned block of 576 rows (0 to 575, 576 to 1151, ..., all dimensions but the last counted through in order) at most 13 rows name the same one
- keep: int32 [8, 64, 576], P('tall', 'wide'), may hold values 0 or 1
Outputs:
- mixed: bfloat16 [192, 1536, 512], P('tall', 'wide')
The draws below stay inside these ranges and needn't reach their ends.
Inputs may be any that keep to these rules, and one draw needn't show every extreme that they name: `expert_ids`: within the tokens of one tile (one index of the first two dimensions), no expert is named more than 13 times, a bound that some block reaches.
All inputs are finite; a program needn't handle non-finite values. No bound on the sum of `keep` on one device may be relied on, other than what follows from the above.
Results may differ from the reference program's by a relative error of at most 0.012.
The reference program's roundings to bfloat16 on the way count: a program that leaves them out, or rounds other values in their place, can miss the bound.
Values may be sent and summed in bfloat16 or wider, within the bound.
A program may use at most 64 MiB of HBM per device.

```python
import math
import jax
import jax.numpy as jnp
import numpy as np
from jax import lax

D = 512
HEADS = 16
HID = 2048
WIN = 24
TILE_H = 24
HEAD_DIM = 32
SHIFT = 12
TOK_DEV = 576
NH = 192
NW = 1536
EXPERTS = 64
CAP = 13
N_WIDE = 64
N_TALL = 8


def plant(values, key, least, high):
    extent = values.shape
    place = [jax.random.randint(jax.random.fold_in(key, axis), (), 0, extent[axis]) for axis in range(len(extent))]
    values = values.at[tuple(place)].set(least)
    longest = extent.index(max(extent))
    place[longest] = (place[longest] + 1) % extent[longest]
    return values.at[tuple(place)].set(high)


def shard_levels(key, extent, split, smallest, high):
    level, own = 1.0, jax.random.fold_in(key, 6)
    for position, parts in split:
        draws = jnp.exp(jax.random.uniform(jax.random.fold_in(own, position), (parts,), jnp.float32, smallest / len(split), high / len(split)))
        level = level * jnp.repeat(draws, extent[position] // parts).reshape([-1 if axis == position else 1 for axis in range(len(extent))])
    return level


def shared_out(own_key, own, number, rows, number_of, top, bound, lean):
    order = jax.random.permutation(own_key, number_of)
    crowded, ordinary = load_shares(number_of, rows * top, bound, lean, True), load_shares(number_of, rows * top, bound, lean, False)
    places = jnp.arange(number_of)

    def named(lengths, offset_by):
        used = int((lengths > 0).sum())
        fixed = max(1, used // 4)
        passed = fixed + (places - fixed + offset_by * (used - fixed)) % max(1, number_of - fixed)
        return jnp.zeros((number_of,), jnp.int32).at[order[jnp.where(places < fixed, places, passed)]].set(jnp.asarray(lengths, jnp.int32))

    lengths = jnp.where(number % 4 == 0, named(crowded, number // 4), named(ordinary, number - number // 4 - 1))
    mixed = jax.random.permutation(jax.random.fold_in(own, 3), number_of)
    source_of, receiver = mixed[0:number_of // 2 * 2:2], mixed[1:number_of // 2 * 2:2]
    margin = jnp.minimum(lengths[source_of] - 1, bound - lengths[receiver]) // 2
    margin = jnp.where((source_of == order[0]) | (receiver == order[0]) | (lengths[receiver] == 0), 0, jnp.maximum(margin, 0))
    passed = jax.random.randint(jax.random.fold_in(own, 4), (number_of // 2,), 0, 1 << 20) % (margin + 1)
    lengths = lengths.at[source_of].add(-passed).at[receiver].add(passed)
    items = jnp.searchsorted(jnp.cumsum(lengths), jnp.arange(rows * top), side="right").astype(jnp.int32)
    listing = items.reshape(top, rows).T
    listing = listing[jax.random.permutation(jax.random.fold_in(own, 1), rows)]
    offset_by = jax.random.randint(jax.random.fold_in(own, 2), (rows, 1), 0, top)
    return jnp.take_along_axis(listing, (jnp.arange(top)[None, :] + offset_by) % top, axis=1)


def load_shares(amount, total, most, lean, full):
    portions = [(1 << 20) // math.isqrt(grade ** lean) + 1 for grade in range(1, amount + 1)]
    largest = most if full else min(most, max(-(-total // amount), total * portions[0] // sum(portions)))
    least = 1 if total - largest >= amount - 1 else 0
    given, surplus = [largest] + [least] * (amount - 1), total - largest - least * (amount - 1)
    while surplus > 0:
        candidates = [i for i in range(1, amount) if given[i] < largest] or [i for i in range(1, amount) if given[i] < most]
        mass, remaining = sum([portions[i] for i in candidates]), surplus
        for i in candidates:
            more = min(most - given[i], max(1, remaining * portions[i] // mass), surplus)
            given[i] = given[i] + more
            surplus = surplus - more
    return np.array(given)


def normal_values(stream_key, extent, scale, most, shards=(), held_as=jnp.bfloat16):
    drawn = scale * jax.random.normal(stream_key, extent, jnp.float32)
    if shards:
        drawn = drawn * shard_levels(stream_key, extent, shards, -0.22, 0.18)
    return jnp.clip(drawn, -most, most).astype(held_as)


def setup_inputs(seed: int = 0) -> dict:
    arg_keys = jax.random.split(jax.random.key(seed), 12)
    tokens = normal_values(arg_keys[0], (NH, NW, D), 1.0, 6.0, ((0, 8), (1, 64)))
    qkv_weight = normal_values(arg_keys[1], (D, 3 * D), D ** -0.5, 0.25)
    proj_weight = normal_values(arg_keys[2], (D, D), D ** -0.5, 0.25)
    head_scale = jnp.clip(jnp.exp(jax.random.uniform(arg_keys[3], (HEADS,), jnp.float32, math.log(5.0), math.log(100.0))), 5.0, 100.0)
    attn_gain = jnp.clip(1.0 + 0.1 * jax.random.normal(arg_keys[4], (D,), jnp.float32), 0.5, 1.5)
    router = normal_values(arg_keys[5], (D, EXPERTS), D ** -0.5, 0.25)
    expert_in = normal_values(arg_keys[6], (EXPERTS, D, HID), D ** -0.5, 0.25, ((0, 64), (2, 8)))
    expert_out = normal_values(arg_keys[7], (EXPERTS, HID, D), HID ** -0.5, 0.125, ((0, 64), (1, 8)))
    moe_gain = jnp.clip(1.0 + 0.1 * jax.random.normal(arg_keys[8], (D,), jnp.float32), 0.5, 1.5)
    expert_ids_keys = jax.random.split(jax.random.fold_in(arg_keys[9], 1), N_TALL * N_WIDE * TOK_DEV // TOK_DEV)
    expert_ids_turns = jax.random.permutation(jax.random.fold_in(arg_keys[9], 3), N_TALL * N_WIDE * TOK_DEV // TOK_DEV)
    expert_ids = jax.vmap(lambda own, number: shared_out(jax.random.fold_in(arg_keys[9], 2), own, number, TOK_DEV, EXPERTS, 1, CAP, 2))(expert_ids_keys, expert_ids_turns).reshape((N_TALL, N_WIDE, TOK_DEV, 1))
    keep = plant((jax.random.randint(arg_keys[10], (N_TALL, N_WIDE, TOK_DEV), 0, 8) < 7).astype(jnp.int32), jax.random.fold_in(arg_keys[10], 1), 0, 1)
    return dict(tokens=tokens, qkv_weight=qkv_weight, proj_weight=proj_weight, head_scale=head_scale, attn_gain=attn_gain, router=router, expert_in=expert_in, expert_out=expert_out, moe_gain=moe_gain, expert_ids=expert_ids, keep=keep)


def normalize(values_in, gain_vec):
    average = lax.optimization_barrier(jnp.mean(values_in, axis=-1, keepdims=True))
    centered = values_in - average
    spread = lax.optimization_barrier(jnp.mean(centered * centered, axis=-1, keepdims=True))
    return centered * lax.rsqrt(spread + 1e-05) * gain_vec

def unit_heads(block, head_count):
    shaped = block.reshape(block.shape[0], head_count, -1)
    return (shaped * lax.rsqrt(lax.optimization_barrier(jnp.sum(shaped * shaped, axis=-1, keepdims=True)) + 1e-06)).astype(jnp.bfloat16)

def window_out(window, first_row, first_col, qkv_weight, proj_weight, head_scale, attn_gain):
    window_len = WIN * WIN
    offsets = jnp.arange(window_len, dtype=jnp.int32)
    row_index = first_row + offsets // WIN
    col_index = first_col + offsets % WIN
    region = (row_index + SHIFT >= NH).astype(jnp.int32) * 2 + (col_index + SHIFT >= NW).astype(jnp.int32)
    masking = jnp.where(region[:, None] == region[None, :], 0.0, -100.0).astype(jnp.float32)
    project = jnp.dot(window, qkv_weight, preferred_element_type=jnp.float32)
    queries = unit_heads(project[:, :D], HEADS)
    key_heads = unit_heads(project[:, D:2 * D], HEADS)
    value_heads = project[:, 2 * D:].astype(jnp.bfloat16).reshape(window_len, HEADS, HEAD_DIM)
    scores = jnp.einsum('qhd,khd->hqk', queries.astype(jnp.float32), key_heads.astype(jnp.float32))
    scores = scores * head_scale[:, None, None] + masking[None]
    weights_soft = jax.nn.softmax(scores, axis=-1).astype(jnp.bfloat16)
    attended = jnp.einsum('hqk,khd->qhd', weights_soft.astype(jnp.float32), value_heads.astype(jnp.float32))
    attended = attended.astype(jnp.bfloat16).reshape(window_len, D)
    output = jnp.dot(attended, proj_weight, preferred_element_type=jnp.float32)
    return (window.astype(jnp.float32) + normalize(output, attn_gain)).astype(jnp.bfloat16)

def expert_row(tile_rows, route_ids, keep_flag, router, expert_in, expert_out, moe_gain):
    onehot = (route_ids[..., None] == jnp.arange(EXPERTS, dtype=jnp.int32)).astype(jnp.int32)
    live_hits = onehot * keep_flag[..., None]
    before = jnp.cumsum(live_hits, axis=1) - live_hits
    slot_ids = lax.optimization_barrier(jnp.sum(before * onehot, axis=-1))
    target = jnp.where(keep_flag == 1, route_ids * CAP + slot_ids, EXPERTS * CAP).astype(jnp.int32)
    sources = jnp.broadcast_to(jnp.arange(N_WIDE, dtype=jnp.int32)[:, None], target.shape)
    buffer = jnp.zeros((N_WIDE, EXPERTS * CAP + 1, D), jnp.bfloat16).at[sources, target].set(tile_rows)
    grouped = buffer[:, :EXPERTS * CAP].reshape(N_WIDE, EXPERTS, CAP, D).transpose(1, 0, 2, 3)
    grouped = grouped.reshape(EXPERTS, N_WIDE * CAP, D)
    hidden = jnp.einsum('erd,edh->erh', grouped.astype(jnp.float32), expert_in.astype(jnp.float32))
    hidden = jax.nn.gelu(hidden, approximate=False).astype(jnp.bfloat16)
    produced = jnp.einsum('erh,ehd->erd', hidden.astype(jnp.float32), expert_out.astype(jnp.float32)).astype(jnp.bfloat16)
    back = produced.reshape(EXPERTS, N_WIDE, CAP, D).transpose(1, 0, 2, 3).reshape(N_WIDE, EXPERTS * CAP, D)
    back = jnp.concatenate([back, jnp.zeros((N_WIDE, 1, D), jnp.bfloat16)], axis=1)
    picked = jnp.take_along_axis(back, target[..., None], axis=1)
    logits = jnp.einsum('wtd,de->wte', tile_rows.astype(jnp.float32), router.astype(jnp.float32))
    gate_prob = jax.nn.sigmoid(lax.optimization_barrier(jnp.sum(logits * onehot.astype(jnp.float32), axis=-1)))
    scaled = keep_flag.astype(jnp.float32) * gate_prob
    return (tile_rows.astype(jnp.float32) + scaled[..., None] * normalize(picked.astype(jnp.float32), moe_gain)).astype(jnp.bfloat16)

def reference(tokens, qkv_weight, proj_weight, head_scale, attn_gain, router, expert_in, expert_out, moe_gain, expert_ids, keep):
    rolled = jnp.roll(tokens, (-SHIFT, -SHIFT), axis=(0, 1))
    across = NW // WIN
    windows = rolled.reshape(NH // WIN, WIN, across, WIN, D).transpose(0, 2, 1, 3, 4).reshape(-1, WIN * WIN, D)
    numbers = jnp.arange(windows.shape[0], dtype=jnp.int32)
    first_rows = numbers // across * WIN
    first_cols = numbers % across * WIN
    mixed_in = lax.map(lambda pieces: window_out(pieces[0], pieces[1], pieces[2], qkv_weight, proj_weight, head_scale, attn_gain), (windows, first_rows, first_cols))
    grid = mixed_in.reshape(NH // WIN, across, WIN, WIN, D).transpose(0, 2, 1, 3, 4).reshape(NH, NW, D)
    tiles = grid.reshape(N_TALL, TILE_H, N_WIDE, WIN, D).transpose(0, 2, 1, 3, 4).reshape(N_TALL, N_WIDE, TOK_DEV, D)
    rows_out = lax.map(lambda pieces: expert_row(pieces[0], pieces[1], pieces[2], router, expert_in, expert_out, moe_gain), (tiles, expert_ids[..., 0], keep))
    return rows_out.reshape(N_TALL, N_WIDE, TILE_H, WIN, D).transpose(0, 2, 1, 3, 4).reshape(NH, NW, D)
```

```python
import functools
import math

import jax
import jax.numpy as jnp
from jax import lax
from jax.experimental import pallas as pl
from jax.experimental.pallas import tpu as pltpu
from jax.sharding import PartitionSpec as P

F32, BF16, I32 = jnp.float32, jnp.bfloat16, jnp.int32
MESH = pl.DeviceIdType.MESH
EDGE = 24
HALF = EDGE // 2
TOK = EDGE * EDGE
QUAD = HALF * HALF
HEADS = 16
HEAD = 32
D = 512
GROUP = 4
SPAN = GROUP * TOK
TILE = 256
LOG2E = math.log2(math.e)
CENTRE = 0.375
SAFE = 2.0**-60
ROOM = 16
NT = (((1,), (1,)), ((), ()))
TN = (((0,), (0,)), ((), ()))
VMEM = pl.BlockSpec(memory_space=pltpu.VMEM)
SMEM = pl.BlockSpec(memory_space=pltpu.SMEM)
ANY = pl.BlockSpec(memory_space=pl.ANY)


def dot(a, b, dims=None):
    if dims is None:
        return jnp.dot(a, b, preferred_element_type=F32)
    return lax.dot_general(a, b, dims, preferred_element_type=F32)


def iota(shape, axis):
    return lax.broadcasted_iota(I32, shape, axis)


def norm(value, gain):
    mean = jnp.mean(value, axis=-1, keepdims=True)
    centred = value - mean
    return centred * lax.rsqrt(jnp.mean(centred * centred, axis=-1, keepdims=True) + 1e-5) * gain


def gelu(value):
    size = jnp.abs(value)
    t = 1.0 / (1.0 + (0.3275911 / math.sqrt(2.0)) * size)
    poly = t * (
        0.5 * 0.254829592
        + t * (0.5 * -0.284496736 + t * (0.5 * 1.421413741 + t * (0.5 * -1.453152027 + t * (0.5 * 1.061405429))))
    )
    return jnp.maximum(value, 0.0) - size * poly * jnp.exp2((-0.5 * LOG2E) * (value * value))


def unit(block):
    ones = (iota((TILE, TILE), 0) // HEAD == iota((TILE, TILE), 1) // HEAD).astype(BF16)
    square = block * block
    high = square.astype(BF16)
    low = (square - high.astype(F32)).astype(BF16)
    return (block * lax.rsqrt(dot(high, ones) + dot(low, ones) + 1e-6)).astype(BF16)


def region_column(total_rows, total_cols):
    place = iota((TOK, 1), 0)
    row = lax.axis_index("tall") * EDGE + place // EDGE
    col = lax.axis_index("wide") * EDGE + place % EDGE
    return (row + HALF >= total_rows).astype(I32) * 2 + (col + HALF >= total_cols).astype(I32)


def prepare(x, qkv_ref, scale_ref, region, q_ref, k_ref, v_ref):
    lane = iota((1, 128), 1)
    feat, own_head = lane % HEAD, lane // HEAD
    key_feat = jnp.where(feat < 12, jnp.where(region == feat % 4, 0.0, -1.0), jnp.where(feat == 12, 1.0, 0.0))
    for half in range(2):
        at = TILE * half
        qn = unit(dot(x, qkv_ref[:, at : at + TILE]))
        kn = unit(dot(x, qkv_ref[:, D + at : D + at + TILE]))
        vb = dot(x, qkv_ref[:, 2 * D + at : 2 * D + at + TILE]).astype(BF16)
        for sub in range(2):
            g = 2 * half + sub
            cut = slice(128 * sub, 128 * sub + 128)
            scale = jnp.ones((1, 128), F32)
            for h in range(GROUP):
                scale = jnp.where(own_head == h, scale_ref[g * GROUP + h], scale)
            whole = 100.0 / scale
            high = whole.astype(BF16).astype(F32)
            middle = (whole - high).astype(BF16).astype(F32)
            piece = jnp.where(feat < 4, high, jnp.where(feat < 8, middle, whole - high - middle))
            query_feat = jnp.where(
                feat < 12, jnp.where(region == feat % 4, piece, 0.0), jnp.where(feat == 12, -CENTRE, 0.0)
            )
            q_ref[g, :, 0:128] = qn[:, cut]
            q_ref[g, :, 128:256] = query_feat.astype(BF16)
            for h in range(GROUP):
                mine = own_head == h
                rows = slice(h * TOK, h * TOK + TOK)
                k_ref[g, rows, 0:128] = jnp.where(mine, kn[:, cut], jnp.zeros((), BF16))
                k_ref[g, rows, 128:256] = jnp.where(mine, key_feat, 0.0).astype(BF16)
                v_ref[g, rows, 0:128] = jnp.where(mine, vb[:, cut], jnp.zeros((), BF16))
                v_ref[g, rows, 128:256] = jnp.broadcast_to(jnp.where(mine, 1.0, 0.0), (TOK, 128)).astype(BF16)


def lane_scales(scale_ref, g):
    out = jnp.zeros((1, SPAN), F32)
    for h in range(GROUP):
        out = jnp.where(iota((1, SPAN), 1) // TOK == h, scale_ref[g * GROUP + h] * LOG2E, out)
    return out


def attend(q_ref, k_ref, v_ref, scale_ref, att_ref):
    least = jnp.full((TOK, 128), jnp.inf, F32)
    for g in range(HEADS // GROUP):
        scales = lane_scales(scale_ref, g)
        acc = None
        for j in range(SPAN // TILE):
            at = slice(TILE * j, TILE * j + TILE)
            powers = jnp.exp2(dot(q_ref[g], k_ref[g, at, :], NT) * scales[:, at]).astype(BF16)
            part = dot(powers, v_ref[g, at, :])
            acc = part if acc is None else acc + part
        total = acc[:, 128:]
        least = jnp.minimum(least, total)
        att_ref[:, 128 * g : 128 * g + 128] = (acc[:, :128] / total).astype(BF16)
    return jnp.min(least.reshape(TOK // 8, 8, 128), axis=0)


def attend_exact(q_ref, k_ref, v_ref, scale_ref, att_ref):
    def one(g, carry):
        scales = lane_scales(scale_ref, g)
        owner = iota((1, SPAN), 1) // TOK

        def block(b, carry):
            rows = pl.ds(pl.multiple_of(b * QUAD, QUAD), QUAD)
            score = dot(q_ref[g, rows, :], k_ref[g], NT) * scales
            top = jnp.zeros_like(score)
            for h in range(GROUP):
                peak = jnp.max(jnp.where(owner == h, score, -jnp.inf), axis=-1, keepdims=True)
                top = jnp.where(owner == h, peak, top)
            acc = dot(jnp.exp2(score - top).astype(BF16), v_ref[g])
            att_ref[g, rows, :] = (acc[:, :128] / acc[:, 128:]).astype(BF16)
            return carry

        return lax.fori_loop(0, TOK // QUAD, block, carry)

    lax.fori_loop(0, HEADS // GROUP, one, 0)


def attention_kernel(
    limits, tokens_ref, qkv_hbm, proj_hbm, gain_ref, scale_ref, x_ref, x1_ref, least_ref,
    send, recv, qkv_ref, proj_ref, q_ref, k_ref, v_ref, att_ref, load_sem, send_sem, recv_sem,
):
    tall, wide = lax.axis_index("tall"), lax.axis_index("wide")
    n_tall, n_wide = lax.axis_size("tall"), lax.axis_size("wide")
    loads = [
        pltpu.make_async_copy(qkv_hbm, qkv_ref, load_sem.at[0]),
        pltpu.make_async_copy(proj_hbm, proj_ref, load_sem.at[1]),
    ]
    for load in loads:
        load.start()
    up, left = lax.rem(tall + n_tall - 1, n_tall), lax.rem(wide + n_wide - 1, n_wide)
    down, right = lax.rem(tall + 1, n_tall), lax.rem(wide + 1, n_wide)
    targets = [(left_of, up_of) for left_of, up_of in ((wide, up), (left, tall), (left, up))]
    sources = [(wide, down), (right, tall), (right, down)]
    barrier = pltpu.get_barrier_semaphore()
    for peer in targets + sources:
        pl.semaphore_signal(barrier, inc=1, device_id=peer, device_id_type=MESH)
    place = iota((TOK, TOK), 0)
    quad, rest = place // QUAD, place % QUAD
    row = rest // HALF + jnp.where(quad % 2 == 0, HALF, 0)
    col = rest % HALF + jnp.where(quad < 2, HALF, 0)
    pick = (iota((TOK, TOK), 1) == row * EDGE + col).astype(BF16)
    send[...] = dot(pick, tokens_ref[...]).astype(BF16)
    recv[0:QUAD, :] = send[0:QUAD, :]
    pl.semaphore_wait(barrier, 6)
    copies = []
    for i, peer in enumerate(targets):
        rows = pl.ds(QUAD * (i + 1), QUAD)
        copies.append(
            pltpu.make_async_remote_copy(
                src_ref=send.at[rows], dst_ref=recv.at[rows], send_sem=send_sem.at[i], recv_sem=recv_sem.at[i],
                device_id=peer, device_id_type=MESH,
            )
        )
        copies[-1].start()
    row, col = place // EDGE, place % EDGE
    quad = (row // HALF) + 2 * (col // HALF)
    pick = (iota((TOK, TOK), 1) == quad * QUAD + (row % HALF) * HALF + col % HALF).astype(BF16)
    for load in loads:
        load.wait()
    for copy in copies:
        copy.wait()
    x = dot(pick, recv[...]).astype(BF16)
    x_ref[...] = x
    prepare(x, qkv_ref, scale_ref, region_column(*limits), q_ref, k_ref, v_ref)
    least_ref[...] = attend(q_ref, k_ref, v_ref, scale_ref, att_ref)
    out = dot(att_ref[...], proj_ref[...])
    x1_ref[...] = (x_ref[...].astype(F32) + norm(out, gain_ref[...])).astype(BF16)


def dispatch_kernel(
    limits, experts, x_hbm, x1_in, least_ref, ids_ref, keep_ref, qkv_hbm, proj_hbm, gain_ref, scale_ref,
    x1_ref, slots_ref, target_ref, x_ref, qkv_ref, proj_ref, q_ref, k_ref, v_ref, att_ref,
):
    x1_ref[...] = x1_in[...]

    @pl.when(jnp.logical_not(jnp.min(least_ref[...]) >= SAFE))
    def _():
        pltpu.sync_copy(x_hbm, x_ref)
        pltpu.sync_copy(qkv_hbm, qkv_ref)
        pltpu.sync_copy(proj_hbm, proj_ref)
        prepare(x_ref[...], qkv_ref, scale_ref, region_column(*limits), q_ref, k_ref, v_ref)
        attend_exact(q_ref, k_ref, v_ref, scale_ref, att_ref)
        out = dot(att_ref[0], proj_ref[0:128, :])
        for g in range(1, HEADS // GROUP):
            out += dot(att_ref[g], proj_ref[128 * g : 128 * g + 128, :])
        x1_ref[...] = (x_ref[...].astype(F32) + norm(out, gain_ref[...])).astype(BF16)

    ids, kept = ids_ref[...], keep_ref[...] == 1
    named = iota((experts, TOK), 0) == ids
    live = jnp.where(jnp.logical_and(named, kept), 1.0, 0.0).astype(BF16)
    earlier = (iota((TOK, TOK), 0) < iota((TOK, TOK), 1)).astype(BF16)
    slot = jnp.sum(jnp.where(named, dot(live, earlier), 0.0), axis=0, keepdims=True).astype(I32)
    target = jnp.where(kept, ids * ROOM + slot, -1)
    target_ref[...] = target
    spread = (iota((experts * ROOM, TOK), 0) == target).astype(BF16)
    slots_ref[...] = dot(spread, x1_ref[...]).astype(BF16)


def expert_kernel(
    experts, slots_ref, x1_ref, target_ref, router_ref, gain_ref, in_hbm, out_hbm, result_ref,
    arrived, made, back, acc, spread, gate, w_in, w_out, own_sem, give_sem, take_sem, ring_send, ring_recv,
):
    tall, wide = lax.axis_index("tall"), lax.axis_index("wide")
    n_tall, n_wide = lax.axis_size("tall"), lax.axis_size("wide")
    last = n_tall // 2
    down, up = lax.rem(tall + 1, n_tall), lax.rem(tall + n_tall - 1, n_tall)
    barrier = pltpu.get_barrier_semaphore()

    def partner(k):
        step = (k // 2) % 8
        size = (step + 1) // 2
        dy = size + (step + 1) % 2 * (8 - 2 * size)
        dx, dc = k // 16, k % 2
        core, x, y = wide % 2, (wide // 2) % 4, wide // 8
        return ((y + dy) % 8 * 4 + (x + dx) % 4) * 2 + (core + dc) % 2

    def greet(k, carry):
        pl.semaphore_signal(barrier, inc=1, device_id=(partner(k), tall), device_id_type=MESH)
        return carry

    for peer in (up, down):
        pl.semaphore_signal(barrier, inc=1, device_id=(wide, peer), device_id_type=MESH)
    lax.fori_loop(1, n_wide, greet, 0)
    own = [
        pltpu.make_async_copy(in_hbm, w_in.at[tall], own_sem.at[0]),
        pltpu.make_async_copy(out_hbm, w_out.at[tall], own_sem.at[1]),
        pltpu.make_async_copy(slots_ref.at[pl.ds(wide * ROOM, ROOM)], arrived.at[pl.ds(wide * ROOM, ROOM)], own_sem.at[2]),
    ]
    for copy in own:
        copy.start()
    pl.semaphore_wait(barrier, n_wide + 1)

    def hop(way, step, kind):
        owner = lax.rem(tall + n_tall + (1 - step if way == 0 else step - 1), n_tall)
        whole = (w_in, w_out)[kind].at[owner]
        return pltpu.make_async_remote_copy(
            src_ref=(in_hbm, out_hbm)[kind] if step == 1 else whole,
            dst_ref=whole,
            send_sem=ring_send.at[way, step - 1, kind],
            recv_sem=ring_recv.at[way, step - 1, kind],
            device_id=(wide, down if way == 0 else up),
            device_id_type=MESH,
        )

    def pieces(step):
        return [(0, 0), (1, 1)] if step == last else [(0, 0), (1, 0), (0, 1), (1, 1)]

    hops = {}
    def launch(step):
        for way, kind in pieces(step):
            hops[step, way, kind] = hop(way, step, kind)
            hops[step, way, kind].start()

    def arrive(step):
        for way, kind in pieces(step):
            hops[step, way, kind].wait_recv()

    def exchange(source, landing, phase):
        def one(k, carry):
            peer = partner(k)
            pltpu.make_async_remote_copy(
                src_ref=source.at[pl.ds(pl.multiple_of(peer * ROOM, ROOM), ROOM)],
                dst_ref=landing.at[pl.ds(pl.multiple_of(wide * ROOM, ROOM), ROOM)],
                send_sem=give_sem.at[phase],
                recv_sem=take_sem.at[phase],
                device_id=(peer, tall),
                device_id_type=MESH,
            ).start()
            return carry

        lax.fori_loop(1, n_wide, one, 0)

    def all_of(source, landing, phase):
        rows = pl.ds(0, (n_wide - 1) * ROOM)
        return pltpu.make_async_remote_copy(
            src_ref=source.at[rows], dst_ref=landing.at[rows], send_sem=give_sem.at[phase],
            recv_sem=take_sem.at[phase], device_id=(wide, down), device_id_type=MESH,
        )

    launch(1)
    exchange(slots_ref, arrived, 0)

    target = target_ref[...]
    spread[...] = (iota((experts * ROOM, TOK), 0) == target).astype(BF16)
    live = (iota((experts, TOK), 0) == target // ROOM).astype(BF16)
    eye = (iota((experts, experts), 0) == iota((experts, experts), 1)).astype(BF16)
    chosen = dot(live, eye, TN)
    logit = jnp.sum(dot(x1_ref[...], router_ref[...]) * chosen, axis=-1, keepdims=True)
    kept = jnp.sum(chosen, axis=-1, keepdims=True)
    gate[...] = jnp.broadcast_to(kept * jax.nn.sigmoid(logit), gate.shape)

    def chunk(owner, first=False):
        def rows(b, carry):
            at = pl.ds(pl.multiple_of(b * TILE, TILE), TILE)
            hidden = gelu(dot(arrived[at, :], w_in[owner])).astype(BF16)
            part = dot(hidden, w_out[owner])
            acc[at, :] = part if first else acc[at, :] + part
            return carry

        lax.fori_loop(0, experts * ROOM // TILE, rows, 0)

    arrive(1)
    launch(2)
    for copy in own:
        copy.wait()
    all_of(slots_ref, arrived, 0).wait_recv()
    chunk(tall, True)
    chunk(lax.rem(tall + n_tall - 1, n_tall))
    chunk(lax.rem(tall + 1, n_tall))
    for step in range(2, last + 1):
        arrive(step)
        if step < last:
            launch(step + 1)
            chunk(lax.rem(tall + n_tall - step, n_tall))
        chunk(lax.rem(tall + step, n_tall))
    made[...] = acc[...].astype(BF16)
    mine = pltpu.make_async_copy(
        made.at[pl.ds(wide * ROOM, ROOM)], back.at[pl.ds(wide * ROOM, ROOM)], own_sem.at[2]
    )
    mine.start()
    exchange(made, back, 1)
    mine.wait()
    all_of(slots_ref, arrived, 0).wait_send()
    for copy in hops.values():
        copy.wait_send()
    all_of(made, back, 1).wait_recv()
    picked = dot(spread[...], back[...], TN)
    result_ref[...] = (
        x1_ref[...].astype(F32) + gate[:, 0:1] * norm(picked, gain_ref[...])
    ).astype(BF16)
    all_of(made, back, 1).wait_send()


def body(
    tokens, qkv_weight, proj_weight, head_scale, attn_gain, router, expert_in, expert_out, moe_gain, expert_ids, keep
):
    n_tall, n_wide = lax.axis_size("tall"), lax.axis_size("wide")
    experts = router.shape[1]
    limits = (EDGE * n_tall, EDGE * n_wide)
    hidden = expert_in.shape[2]
    grid_shape = jax.ShapeDtypeStruct((TOK, D), BF16)
    qkv_scratch = [
        pltpu.VMEM((D, 3 * D), BF16),
        pltpu.VMEM((D, D), BF16),
        pltpu.VMEM((HEADS // GROUP, TOK, TILE), BF16),
        pltpu.VMEM((HEADS // GROUP, SPAN, TILE), BF16),
        pltpu.VMEM((HEADS // GROUP, SPAN, TILE), BF16),
    ]
    DMA = pltpu.SemaphoreType.DMA
    x, x1, least = pl.pallas_call(
        functools.partial(attention_kernel, limits),
        out_shape=(grid_shape, grid_shape, jax.ShapeDtypeStruct((8, 128), F32)),
        in_specs=[VMEM, ANY, ANY, VMEM, SMEM],
        out_specs=(VMEM, VMEM, VMEM),
        scratch_shapes=[pltpu.VMEM((TOK, D), BF16), pltpu.VMEM((TOK, D), BF16)]
        + qkv_scratch
        + [pltpu.VMEM((TOK, D), BF16), DMA((2,)), DMA((3,)), DMA((3,))],
        compiler_params=pltpu.CompilerParams(collective_id=0, has_side_effects=True, vmem_limit_bytes=50 << 20),
        name="attention",
    )(tokens.reshape(TOK, D), qkv_weight, proj_weight, attn_gain.reshape(1, D), head_scale)
    slot_shape = jax.ShapeDtypeStruct((experts * ROOM, D), BF16)
    x1, slots, target = pl.pallas_call(
        functools.partial(dispatch_kernel, limits, experts),
        out_shape=(grid_shape, slot_shape, jax.ShapeDtypeStruct((1, TOK), I32)),
        in_specs=[ANY, VMEM, VMEM, VMEM, VMEM, ANY, ANY, VMEM, SMEM],
        out_specs=(VMEM, VMEM, VMEM),
        scratch_shapes=[pltpu.VMEM((TOK, D), BF16)]
        + qkv_scratch
        + [pltpu.VMEM((HEADS // GROUP, TOK, 128), BF16)],
        compiler_params=pltpu.CompilerParams(vmem_limit_bytes=50 << 20),
        name="dispatch",
    )(
        x, x1, least, expert_ids.reshape(1, TOK), keep.reshape(1, TOK), qkv_weight, proj_weight,
        attn_gain.reshape(1, D), head_scale,
    )
    slot_buffer = pltpu.VMEM((experts * ROOM, D), BF16)
    out = pl.pallas_call(
        functools.partial(expert_kernel, experts),
        out_shape=grid_shape,
        in_specs=[VMEM, VMEM, VMEM, VMEM, VMEM, ANY, ANY],
        out_specs=VMEM,
        scratch_shapes=[
            slot_buffer,
            slot_buffer,
            slot_buffer,
            pltpu.VMEM((experts * ROOM, D), F32),
            pltpu.VMEM((experts * ROOM, TOK), BF16),
            pltpu.VMEM((TOK, 128), F32),
            pltpu.VMEM((n_tall, D, hidden), BF16),
            pltpu.VMEM((n_tall, hidden, D), BF16),
            DMA((3,)),
            DMA((2,)),
            DMA((2,)),
            DMA((2, n_tall // 2, 2)),
            DMA((2, n_tall // 2, 2)),
        ],
        compiler_params=pltpu.CompilerParams(collective_id=1, has_side_effects=True, vmem_limit_bytes=50 << 20),
        name="experts",
    )(slots, x1, target, router, moe_gain.reshape(1, D), expert_in[0], expert_out[0])
    return out.reshape(EDGE, EDGE, D)


def solution(mesh):
    placed = (
        P("tall", "wide", None), P(), P(), P(), P(), P(), P("wide", None, "tall"), P("wide", "tall", None), P(),
        P("tall", "wide", None, None), P("tall", "wide", None),
    )
    return jax.shard_map(
        body, mesh=mesh, in_specs=placed, out_specs=P("tall", "wide", None), check_vma=False
    )
```

```python
import functools
import math

import jax
import jax.numpy as jnp
from jax import lax
from jax.experimental import pallas as pl
from jax.experimental.pallas import tpu as pltpu
from jax.sharding import PartitionSpec as P

F32, BF16, I32 = jnp.float32, jnp.bfloat16, jnp.int32
MESH = pl.DeviceIdType.MESH
EDGE = 24
HALF = EDGE // 2
TOK = EDGE * EDGE
QUAD = HALF * HALF
HEADS = 16
HEAD = 32
D = 512
GROUP = 4
SPAN = GROUP * TOK
TILE = 256
LOG2E = math.log2(math.e)
CENTRE = 0.375
SAFE = 2.0**-60
ROOM = 13
LANES = 128
WAYS = D // LANES
NT = (((1,), (1,)), ((), ()))
TN = (((0,), (0,)), ((), ()))
VMEM = pl.BlockSpec(memory_space=pltpu.VMEM)
SMEM = pl.BlockSpec(memory_space=pltpu.SMEM)
HBM = pl.BlockSpec(memory_space=pltpu.HBM)


def dot(a, b, dims=None):
    if dims is None:
        return jnp.dot(a, b, preferred_element_type=F32)
    return lax.dot_general(a, b, dims, preferred_element_type=F32)


def iota(shape, axis):
    return lax.broadcasted_iota(I32, shape, axis)


def norm(value, gain):
    mean = jnp.mean(value, axis=-1, keepdims=True)
    centred = value - mean
    return centred * lax.rsqrt(jnp.mean(centred * centred, axis=-1, keepdims=True) + 1e-5) * gain


def gelu(value):
    return 0.5 * value * (1.0 + lax.erf(value * math.sqrt(0.5)))


def unit(block):
    ones = (iota((TILE, TILE), 0) // HEAD == iota((TILE, TILE), 1) // HEAD).astype(BF16)
    square = block * block
    high = square.astype(BF16)
    low = (square - high.astype(F32)).astype(BF16)
    return (block * lax.rsqrt(dot(high, ones) + dot(low, ones) + 1e-6)).astype(BF16)


def region_column(total_rows, total_cols):
    place = iota((TOK, 1), 0)
    row = lax.axis_index("tall") * EDGE + place // EDGE
    col = lax.axis_index("wide") * EDGE + place % EDGE
    return (row + HALF >= total_rows).astype(I32) * 2 + (col + HALF >= total_cols).astype(I32)


def features(scale_ref, region, q_ref, k_ref, v_ref):
    lane = iota((1, 128), 1)
    feat, own_head = lane % HEAD, lane // HEAD
    key_feat = jnp.where(feat < 12, jnp.where(region == feat % 4, 0.0, -1.0), jnp.where(feat == 12, 1.0, 0.0))
    for g in range(HEADS // GROUP):
        scale = jnp.ones((1, 128), F32)
        for h in range(GROUP):
            scale = jnp.where(own_head == h, scale_ref[g * GROUP + h], scale)
        whole = 100.0 / scale
        high = whole.astype(BF16).astype(F32)
        middle = (whole - high).astype(BF16).astype(F32)
        piece = jnp.where(feat < 4, high, jnp.where(feat < 8, middle, whole - high - middle))
        query_feat = jnp.where(
            feat < 12, jnp.where(region == feat % 4, piece, 0.0), jnp.where(feat == 12, -CENTRE, 0.0)
        )
        q_ref[g, :, 128:256] = query_feat.astype(BF16)
        for h in range(GROUP):
            mine = own_head == h
            rows = slice(h * TOK, h * TOK + TOK)
            k_ref[g, rows, 128:256] = jnp.where(mine, key_feat, 0.0).astype(BF16)
            v_ref[g, rows, 128:256] = jnp.broadcast_to(jnp.where(mine, 1.0, 0.0), (TOK, 128)).astype(BF16)


def prepare(x, qkv_ref, q_ref, k_ref, v_ref):
    own_head = iota((1, 128), 1) // HEAD
    for half in range(2):
        at = TILE * half
        qn = unit(dot(x, qkv_ref[:, at : at + TILE]))
        kn = unit(dot(x, qkv_ref[:, D + at : D + at + TILE]))
        vb = dot(x, qkv_ref[:, 2 * D + at : 2 * D + at + TILE]).astype(BF16)
        for sub in range(2):
            g = 2 * half + sub
            cut = slice(128 * sub, 128 * sub + 128)
            q_ref[g, :, 0:128] = qn[:, cut]
            for h in range(GROUP):
                mine = own_head == h
                rows = slice(h * TOK, h * TOK + TOK)
                k_ref[g, rows, 0:128] = jnp.where(mine, kn[:, cut], jnp.zeros((), BF16))
                v_ref[g, rows, 0:128] = jnp.where(mine, vb[:, cut], jnp.zeros((), BF16))


def lane_scales(scale_ref, g):
    out = jnp.zeros((1, SPAN), F32)
    for h in range(GROUP):
        out = jnp.where(iota((1, SPAN), 1) // TOK == h, scale_ref[g * GROUP + h] * LOG2E, out)
    return out


def attend(q_ref, k_ref, v_ref, scale_ref, att_ref, between):
    least = jnp.full((TOK, 128), jnp.inf, F32)
    for g in range(HEADS // GROUP):
        scales = lane_scales(scale_ref, g)
        acc = None
        for j in range(SPAN // TILE):
            at = slice(TILE * j, TILE * j + TILE)
            powers = jnp.exp2(dot(q_ref[g], k_ref[g, at, :], NT) * scales[:, at]).astype(BF16)
            part = dot(powers, v_ref[g, at, :])
            acc = part if acc is None else acc + part
        total = acc[:, 128:]
        least = jnp.minimum(least, total)
        att_ref[:, 128 * g : 128 * g + 128] = (acc[:, :128] / total).astype(BF16)
        between(g)
    return jnp.min(least.reshape(TOK // 8, 8, 128), axis=0)


def attend_exact(q_ref, k_ref, v_ref, scale_ref, att_ref):
    def one(g, carry):
        scales = lane_scales(scale_ref, g)
        owner = iota((1, SPAN), 1) // TOK

        def block(b, carry):
            rows = pl.ds(pl.multiple_of(b * QUAD, QUAD), QUAD)
            score = dot(q_ref[g, rows, :], k_ref[g], NT) * scales
            top = jnp.zeros_like(score)
            for h in range(GROUP):
                peak = jnp.max(jnp.where(owner == h, score, -jnp.inf), axis=-1, keepdims=True)
                top = jnp.where(owner == h, peak, top)
            acc = dot(jnp.exp2(score - top).astype(BF16), v_ref[g])
            att_ref[g, rows, :] = (acc[:, :128] / acc[:, 128:]).astype(BF16)
            return carry

        return lax.fori_loop(0, TOK // QUAD, block, carry)

    lax.fori_loop(0, HEADS // GROUP, one, 0)


def ring_hop(own, gathered, way, step, send_sem, recv_sem):
    tall, wide, n_tall = lax.axis_index("tall"), lax.axis_index("wide"), lax.axis_size("tall")
    owner = lax.rem(tall + n_tall + (1 - step if way == 0 else step - 1), n_tall)
    return pltpu.make_async_remote_copy(
        src_ref=own if step == 1 else gathered.at[owner],
        dst_ref=gathered.at[owner],
        send_sem=send_sem.at[way, step - 1],
        recv_sem=recv_sem.at[way, step - 1],
        device_id=(wide, lax.rem(tall + (1 if way == 0 else n_tall - 1), n_tall)),
        device_id_type=MESH,
    )


def attention_kernel(
    limits, tokens_hbm, qkv_hbm, proj_hbm, gain_ref, scale_ref, in_hbm, x_ref, x1_ref, least_ref, w_in,
    tokens_ref, send, recv, qkv_ref, proj_ref, q_ref, k_ref, v_ref, att_ref, load_sem, send_sem, recv_sem,
    ring_send, ring_recv,
):
    tall, wide = lax.axis_index("tall"), lax.axis_index("wide")
    n_tall, n_wide = lax.axis_size("tall"), lax.axis_size("wide")
    loads = [
        pltpu.make_async_copy(tokens_hbm, tokens_ref, load_sem.at[0]),
        pltpu.make_async_copy(qkv_hbm, qkv_ref, load_sem.at[1]),
        pltpu.make_async_copy(proj_hbm, proj_ref, load_sem.at[2]),
        pltpu.make_async_copy(in_hbm, w_in.at[tall], load_sem.at[3]),
    ]
    for load in loads:
        load.start()
    up, left = lax.rem(tall + n_tall - 1, n_tall), lax.rem(wide + n_wide - 1, n_wide)
    down, right = lax.rem(tall + 1, n_tall), lax.rem(wide + 1, n_wide)
    targets = [(wide, up), (left, tall), (left, up)]
    sources = [(wide, down), (right, tall), (right, down)]
    barrier = pltpu.get_barrier_semaphore()
    for peer in targets + sources:
        pl.semaphore_signal(barrier, inc=1, device_id=peer, device_id_type=MESH)
    place = iota((TOK, TOK), 0)
    quad, rest = place // QUAD, place % QUAD
    row = rest // HALF + jnp.where(quad % 2 == 0, HALF, 0)
    col = rest % HALF + jnp.where(quad < 2, HALF, 0)
    pick = (iota((TOK, TOK), 1) == row * EDGE + col).astype(BF16)
    loads[0].wait()
    send[...] = dot(pick, tokens_ref[...]).astype(BF16)
    pl.semaphore_wait(barrier, 6)
    copies = []
    for i, peer in enumerate(targets):
        rows = pl.ds(QUAD * (i + 1), QUAD)
        copies.append(
            pltpu.make_async_remote_copy(
                src_ref=send.at[rows], dst_ref=recv.at[rows], send_sem=send_sem.at[i], recv_sem=recv_sem.at[i],
                device_id=peer, device_id_type=MESH,
            )
        )
        copies[-1].start()
    hops = {}

    def launch(way, step):
        hops[way, step] = ring_hop(in_hbm, w_in, way, step, ring_send, ring_recv)
        hops[way, step].start()

    def onward(way, step):
        hops[way, step].wait_recv()
        launch(way, step + 1)

    launch(0, 1)
    recv[0:QUAD, :] = send[0:QUAD, :]
    row, col = place // EDGE, place % EDGE
    quad = (row // HALF) + 2 * (col // HALF)
    pick = (iota((TOK, TOK), 1) == quad * QUAD + (row % HALF) * HALF + col % HALF).astype(BF16)
    features(scale_ref, region_column(*limits), q_ref, k_ref, v_ref)
    for load in loads[1:]:
        load.wait()
    for copy in copies:
        copy.wait()
    launch(1, 1)
    onward(0, 1)
    x = dot(pick, recv[...]).astype(BF16)
    x_ref[...] = x
    prepare(x, qkv_ref, q_ref, k_ref, v_ref)

    def between(g):
        if g == 1:
            onward(1, 1)
            onward(0, 2)

    least_ref[...] = attend(q_ref, k_ref, v_ref, scale_ref, att_ref, between)
    out = dot(att_ref[...], proj_ref[...])
    x1_ref[...] = (x_ref[...].astype(F32) + norm(out, gain_ref[...])).astype(BF16)
    hops[1, 2].wait_recv()
    hops[0, 3].wait_recv()
    for hop in hops.values():
        hop.wait_send()


def rem(a, n):
    return lax.rem(a, jnp.int32(n))


def div(a, n):
    return lax.div(a, jnp.int32(n))


def partner(k, sign):
    wide = lax.axis_index("wide")
    core, x, y = rem(wide, 2), rem(div(wide, 2), 4), div(wide, 8)
    turn = rem(64 - k, 64)
    step = rem(turn, 8)
    size = div(step + 1, 2)
    dy = size + rem(step + 1, 2) * (8 - 2 * size)
    dx, dc = rem(div(turn, 8), 4), div(turn, 32)
    return (rem(y + 8 + sign * dy, 8) * 4 + rem(x + 4 + sign * dx, 4)) * 2 + rem(core + 2 + sign * dc, 2)


def place_of(expert):
    wide = lax.axis_index("wide")
    dc = (expert % 2 + 2 - wide % 2) % 2
    dx = (expert // 2 % 4 + 4 - wide // 2 % 4) % 4
    dy = (expert // 8 + 8 - wide // 8) % 8
    step = jnp.where(dy == 0, 0, jnp.where(dy <= 4, 2 * dy - 1, 16 - 2 * dy))
    return (64 - (dc * 32 + dx * 8 + step)) % 64


def dispatch_kernel(
    limits, experts, x_hbm, x1_in, least_ref, ids_ref, keep_ref, qkv_hbm, proj_hbm, gain_ref, scale_ref,
    x1_ref, slots_ref, target_ref, x_ref, qkv_ref, proj_ref, q_ref, k_ref, v_ref, att_ref,
):
    x1_ref[...] = x1_in[...]

    @pl.when(jnp.logical_not(jnp.min(least_ref[...]) >= SAFE))
    def _():
        pltpu.sync_copy(x_hbm, x_ref)
        pltpu.sync_copy(qkv_hbm, qkv_ref)
        pltpu.sync_copy(proj_hbm, proj_ref)
        features(scale_ref, region_column(*limits), q_ref, k_ref, v_ref)
        prepare(x_ref[...], qkv_ref, q_ref, k_ref, v_ref)
        attend_exact(q_ref, k_ref, v_ref, scale_ref, att_ref)
        out = dot(att_ref[0], proj_ref[0:128, :])
        for g in range(1, HEADS // GROUP):
            out += dot(att_ref[g], proj_ref[128 * g : 128 * g + 128, :])
        x1_ref[...] = (x_ref[...].astype(F32) + norm(out, gain_ref[...])).astype(BF16)

    ids, kept = ids_ref[...], keep_ref[...] == 1
    named = iota((experts, TOK), 0) == ids
    live = jnp.where(jnp.logical_and(named, kept), 1.0, 0.0).astype(BF16)
    earlier = (iota((TOK, TOK), 0) < iota((TOK, TOK), 1)).astype(BF16)
    slot = jnp.sum(jnp.where(named, dot(live, earlier), 0.0), axis=0, keepdims=True).astype(I32)
    target = jnp.where(kept, place_of(ids) * ROOM + slot, -1)
    target_ref[...] = target
    spread = (iota((experts * ROOM, TOK), 0) == target).astype(BF16)
    slots_ref[...] = dot(spread, x1_ref[...]).astype(BF16).reshape(experts * ROOM, WAYS, LANES)


def expert_kernel(
    experts, slots_ref, x1_ref, target_ref, ids_ref, router_ref, gain_ref, w_in_hbm, out_hbm, result_ref,
    arrived, made, back, hidden, picked, spread, gate, w_in, w_out, own_sem, give_send, give_recv, take_send, take_recv,
    in_send, in_recv, out_send, out_recv,
):
    tall, wide = lax.axis_index("tall"), lax.axis_index("wide")
    n_tall, n_wide = lax.axis_size("tall"), lax.axis_size("wide")
    last = n_tall // 2
    down, up = lax.rem(tall + 1, n_tall), lax.rem(tall + n_tall - 1, n_tall)
    barrier = pltpu.get_barrier_semaphore()

    def greet(k, carry):
        pl.semaphore_signal(barrier, inc=1, device_id=(rem(wide + k, n_wide), tall), device_id_type=MESH)
        return carry

    for peer in (up, down):
        pl.semaphore_signal(barrier, inc=1, device_id=(wide, peer), device_id_type=MESH)
    lax.fori_loop(1, n_wide, greet, 0)
    own = [pltpu.make_async_copy(out_hbm, w_out.at[tall], own_sem.at[0])]
    own.append(pltpu.make_async_copy(slots_ref.at[pl.ds(0, ROOM)], arrived.at[pl.ds(0, ROOM)], own_sem.at[1]))
    for i in range(1 - last, last - 1):
        block = lax.rem(tall + n_tall + i, n_tall)
        own.append(pltpu.make_async_copy(w_in_hbm.at[block], w_in.at[block], own_sem.at[2 + last + i]))
    for copy in own:
        copy.start()
    pl.semaphore_wait(barrier, n_wide + 1)

    hops, sent = {}, []

    def launch(step):
        for way in range(2):
            hops[step, way] = ring_hop(out_hbm, w_out, way, step, out_send, out_recv)
            hops[step, way].start()
            sent.append(hops[step, way])

    def arrive(step):
        for way in range(2):
            hops[step, way].wait_recv()

    def halfway():
        copies = []
        for way in range(2):
            owner = lax.rem(tall + (n_tall + 1 - last if way == 0 else last - 1), n_tall)
            rows = pl.ds(TILE // 2 * way, TILE // 2)
            copies.append(
                pltpu.make_async_remote_copy(
                    src_ref=w_out.at[owner, rows], dst_ref=w_out.at[owner, rows], send_sem=out_send.at[way, last - 1],
                    recv_sem=out_recv.at[way, last - 1], device_id=(wide, down if way == 0 else up),
                    device_id_type=MESH,
                )
            )
            copies[-1].start()
        sent.extend(copies)
        return copies

    def remainder(way):
        owner = lax.rem(tall + (n_tall + 1 - last if way == 0 else last - 2), n_tall)
        copy = pltpu.make_async_remote_copy(
            src_ref=w_in_hbm.at[owner], dst_ref=w_in.at[owner], send_sem=in_send.at[way], recv_sem=in_recv.at[way],
            device_id=(wide, down if way == 0 else up), device_id_type=MESH,
        )
        copy.start()
        sent.append(copy)
        return copy

    def exchange(source, landing, send_sem, recv_sem, sign, start, stop, group):
        def one(k, carry):
            rows = pl.ds(k * ROOM, ROOM)
            pltpu.make_async_remote_copy(
                src_ref=source.at[rows], dst_ref=landing.at[rows], send_sem=send_sem, recv_sem=recv_sem.at[group],
                device_id=(partner(k, sign), tall), device_id_type=MESH,
            ).start()
            return carry

        lax.fori_loop(start, stop, one, 0)

    def whole_of(ref, blocks, send_sem, recv_sem):
        rows = pl.ds(0, blocks * ROOM)
        return pltpu.make_async_remote_copy(
            src_ref=ref.at[rows], dst_ref=ref.at[rows], send_sem=send_sem, recv_sem=recv_sem,
            device_id=(wide, down), device_id_type=MESH,
        )

    per = 8
    groups = n_wide // per
    in_rest = [remainder(0), remainder(1)]
    launch(1)
    for group in range(groups):
        exchange(slots_ref, arrived, give_send.at[0], give_recv, 1, max(1, group * per), group * per + per, group)

    target = target_ref[...]
    live = jnp.where(jnp.logical_and(iota((experts, TOK), 0) == ids_ref[...], target >= 0), 1.0, 0.0)
    eye = (iota((experts, experts), 0) == iota((experts, experts), 1)).astype(BF16)
    chosen = dot(live.astype(BF16), eye, TN)
    slot = (jnp.maximum(target, 0) % ROOM).astype(F32)
    slot = jnp.sum(dot((live * slot).astype(BF16), eye, TN), axis=-1, keepdims=True)
    block = jnp.sum(chosen * place_of(iota((1, experts), 1)).astype(F32), axis=-1, keepdims=True)
    kept = jnp.sum(chosen, axis=-1, keepdims=True)
    landing = jnp.where(kept > 0.5, block * ROOM + slot, -1.0).astype(I32)
    span = 2 * per * ROOM
    for pair in range(groups // 2):
        spread[pair] = (iota((TOK, span), 1) + pair * span == landing).astype(BF16)
    logit = jnp.sum(dot(x1_ref[...], router_ref[...], NT) * chosen, axis=-1, keepdims=True)
    gate[...] = jnp.broadcast_to(kept * jax.nn.sigmoid(logit), gate.shape)

    def first(group):
        rows = slice(group * per * ROOM, (group + 1) * per * ROOM)
        whole_of(arrived, per - (group == 0), give_send.at[0], give_recv.at[group]).wait_recv()
        here = arrived[rows].reshape(per * ROOM, D)
        for c in range(n_tall):
            hidden[group, :, c * TILE : c * TILE + TILE] = gelu(dot(here, w_in[c])).astype(BF16)

    def second(group):
        rows = slice(group * per * ROOM, (group + 1) * per * ROOM)
        out = dot(hidden[group], w_out[...].reshape(n_tall * TILE, D)).astype(BF16)
        made[rows] = out.reshape(per * ROOM, WAYS, LANES)
        exchange(made, back, take_send.at[0], take_recv, -1, max(1, group * per), group * per + per, group)

    for copy in own:
        copy.wait()
    for copy in in_rest:
        copy.wait_recv()
    arrive(1)
    launch(2)
    for group in range(0, 2):
        first(group)
    arrive(2)
    launch(3)
    for group in range(2, 5):
        first(group)
    arrive(3)
    out_far = halfway()
    for group in range(5, groups):
        first(group)
    for copy in out_far:
        copy.wait_recv()
    for group in range(groups):
        second(group)
    mine = pltpu.make_async_copy(made.at[pl.ds(0, ROOM)], back.at[pl.ds(0, ROOM)], own_sem.at[1])
    mine.start()
    for copy in sent:
        copy.wait_send()
    whole_of(slots_ref, n_wide - 1, give_send.at[0], give_recv.at[0]).wait_send()
    mine.wait()
    for pair in range(groups // 2):
        for group in (2 * pair, 2 * pair + 1):
            whole_of(back, per - (group == 0), take_send.at[0], take_recv.at[group]).wait_recv()
        part = dot(spread[pair], back[pair * span : pair * span + span].reshape(span, D))
        if pair < groups // 2 - 1:
            picked[...] = part if pair == 0 else picked[...] + part
    result_ref[...] = (
        x1_ref[...].astype(F32) + gate[:, 0:1] * norm(picked[...] + part, gain_ref[...])
    ).astype(BF16)
    whole_of(made, n_wide - 1, take_send.at[0], take_recv.at[0]).wait_send()


def body(
    tokens, qkv_weight, proj_weight, head_scale, attn_gain, router, expert_in, expert_out, moe_gain, expert_ids, keep
):
    n_tall, n_wide = lax.axis_size("tall"), lax.axis_size("wide")
    experts = router.shape[1]
    limits = (EDGE * n_tall, EDGE * n_wide)
    hidden = expert_in.shape[2]
    grid_shape = jax.ShapeDtypeStruct((TOK, D), BF16)
    qkv_scratch = [
        pltpu.VMEM((D, 3 * D), BF16),
        pltpu.VMEM((D, D), BF16),
        pltpu.VMEM((HEADS // GROUP, TOK, TILE), BF16),
        pltpu.VMEM((HEADS // GROUP, SPAN, TILE), BF16),
        pltpu.VMEM((HEADS // GROUP, SPAN, TILE), BF16),
    ]
    DMA = pltpu.SemaphoreType.DMA
    x, x1, least, w_in = pl.pallas_call(
        functools.partial(attention_kernel, limits),
        out_shape=(
            grid_shape, grid_shape, jax.ShapeDtypeStruct((8, 128), F32), jax.ShapeDtypeStruct((n_tall, D, hidden), BF16)
        ),
        in_specs=[HBM, HBM, HBM, VMEM, SMEM, HBM],
        out_specs=(VMEM, VMEM, VMEM, HBM),
        scratch_shapes=[pltpu.VMEM((TOK, D), BF16)] * 3
        + qkv_scratch
        + [pltpu.VMEM((TOK, D), BF16), DMA((4,)), DMA((3,)), DMA((3,)), DMA((2, 3)), DMA((2, 3))],
        compiler_params=pltpu.CompilerParams(collective_id=0, has_side_effects=True, vmem_limit_bytes=62 << 20),
        name="attention",
    )(tokens.reshape(TOK, D), qkv_weight, proj_weight, attn_gain.reshape(1, D), head_scale, expert_in[0])
    slot_shape = jax.ShapeDtypeStruct((experts * ROOM, WAYS, LANES), BF16)
    ids = expert_ids.reshape(1, TOK)
    x1, slots, target = pl.pallas_call(
        functools.partial(dispatch_kernel, limits, experts),
        out_shape=(grid_shape, slot_shape, jax.ShapeDtypeStruct((1, TOK), I32)),
        in_specs=[HBM, VMEM, VMEM, VMEM, VMEM, HBM, HBM, VMEM, SMEM],
        out_specs=(VMEM, VMEM, VMEM),
        scratch_shapes=[pltpu.VMEM((TOK, D), BF16)]
        + qkv_scratch
        + [pltpu.VMEM((HEADS // GROUP, TOK, 128), BF16)],
        compiler_params=pltpu.CompilerParams(vmem_limit_bytes=62 << 20),
        name="dispatch",
    )(x, x1, least, ids, keep.reshape(1, TOK), qkv_weight, proj_weight, attn_gain.reshape(1, D), head_scale)
    slot_buffer = pltpu.VMEM((experts * ROOM, WAYS, LANES), BF16)
    out = pl.pallas_call(
        functools.partial(expert_kernel, experts),
        out_shape=grid_shape,
        in_specs=[HBM, VMEM, VMEM, VMEM, VMEM, VMEM, HBM, HBM],
        out_specs=VMEM,
        scratch_shapes=[
            slot_buffer,
            slot_buffer,
            slot_buffer,
            pltpu.VMEM((8, experts * ROOM // 8, n_tall * hidden), BF16),
            pltpu.VMEM((TOK, D), F32),
            pltpu.VMEM((4, TOK, experts * ROOM // 4), BF16),
            pltpu.VMEM((TOK, 128), F32),
            pltpu.VMEM((n_tall, D, hidden), BF16),
            pltpu.VMEM((n_tall, hidden, D), BF16),
            DMA((2 + n_tall,)),
            DMA((1,)),
            DMA((8,)),
            DMA((1,)),
            DMA((8,)),
            DMA((2,)),
            DMA((2,)),
            DMA((2, n_tall // 2)),
            DMA((2, n_tall // 2)),
        ],
        compiler_params=pltpu.CompilerParams(collective_id=1, has_side_effects=True, vmem_limit_bytes=62 << 20),
        name="experts",
    )(slots, x1, target, ids, router.T, moe_gain.reshape(1, D), w_in, expert_out[0])
    return out.reshape(EDGE, EDGE, D)


def solution(mesh):
    placed = (
        P("tall", "wide", None), P(), P(), P(), P(), P(), P("wide", None, "tall"), P("wide", "tall", None), P(),
        P("tall", "wide", None, None), P("tall", "wide", None),
    )
    return jax.shard_map(
        body, mesh=mesh, in_specs=placed, out_specs=P("tall", "wide", None), check_vma=False
    )
```

```python
import functools
import math

import jax
import jax.numpy as jnp
from jax import lax
from jax.experimental import pallas as pl
from jax.experimental.pallas import tpu as pltpu
from jax.sharding import PartitionSpec as P

F32, BF16, I32 = jnp.float32, jnp.bfloat16, jnp.int32
MESH = pl.DeviceIdType.MESH
EDGE = 24
HALF = EDGE // 2
TOK = EDGE * EDGE
QUAD = HALF * HALF
HEADS = 16
HEAD = 32
D = 512
GROUP = 4
SPAN = GROUP * TOK
TILE = 256
LOG2E = math.log2(math.e)
ROOM = 13
LANES = 128
WAYS = D // LANES
NT = (((1,), (1,)), ((), ()))
TN = (((0,), (0,)), ((), ()))
VMEM = pl.BlockSpec(memory_space=pltpu.VMEM)
SMEM = pl.BlockSpec(memory_space=pltpu.SMEM)
HBM = pl.BlockSpec(memory_space=pltpu.HBM)


def dot(a, b, dims=None):
    if dims is None:
        return jnp.dot(a, b, preferred_element_type=F32)
    return lax.dot_general(a, b, dims, preferred_element_type=F32)


def iota(shape, axis):
    return lax.broadcasted_iota(I32, shape, axis)


def norm(value, gain):
    mean = jnp.mean(value, axis=-1, keepdims=True)
    centred = value - mean
    return centred * lax.rsqrt(jnp.mean(centred * centred, axis=-1, keepdims=True) + 1e-5) * gain


def gelu(value):
    return 0.5 * value * (1.0 + lax.erf(value * math.sqrt(0.5)))


def unit(block):
    ones = (iota((TILE, TILE), 0) // HEAD == iota((TILE, TILE), 1) // HEAD).astype(BF16)
    square = block * block
    high = square.astype(BF16)
    low = (square - high.astype(F32)).astype(BF16)
    return (block * lax.rsqrt(dot(high, ones) + dot(low, ones) + 1e-6)).astype(BF16)


def region_column(total_rows, total_cols):
    place = iota((TOK, 1), 0)
    row = lax.axis_index("tall") * EDGE + place // EDGE
    col = lax.axis_index("wide") * EDGE + place % EDGE
    return (row + HALF >= total_rows).astype(I32) * 2 + (col + HALF >= total_cols).astype(I32)


def features(scale_ref, region, q_ref, k_ref, v_ref):
    lane = iota((1, 128), 1)
    feat, own_head = lane % HEAD, lane // HEAD
    key_feat = jnp.where(feat < 12, jnp.where(region == feat % 4, 0.0, -1.0), jnp.where(feat == 12, 1.0, 0.0))
    for g in range(HEADS // GROUP):
        scale = jnp.ones((1, 128), F32)
        for h in range(GROUP):
            scale = jnp.where(own_head == h, scale_ref[g * GROUP + h], scale)
        whole = 100.0 / scale
        high = whole.astype(BF16).astype(F32)
        middle = (whole - high).astype(BF16).astype(F32)
        piece = jnp.where(feat < 4, high, jnp.where(feat < 8, middle, whole - high - middle))
        query_feat = jnp.where(jnp.logical_and(feat < 12, region == feat % 4), piece, 0.0)
        q_ref[g, :, 128:256] = query_feat.astype(BF16)
        for h in range(GROUP):
            mine = own_head == h
            rows = slice(h * TOK, h * TOK + TOK)
            k_ref[g, rows, 128:256] = jnp.where(mine, key_feat, 0.0).astype(BF16)
            v_ref[g, rows, 128:256] = jnp.broadcast_to(jnp.where(mine, 1.0, 0.0), (TOK, 128)).astype(BF16)


def prepare(x, qkv_ref, q_ref, k_ref, v_ref):
    own_head = iota((1, 128), 1) // HEAD
    for half in range(2):
        at = TILE * half
        qn = unit(dot(x, qkv_ref[:, at : at + TILE]))
        kn = unit(dot(x, qkv_ref[:, D + at : D + at + TILE]))
        vb = dot(x, qkv_ref[:, 2 * D + at : 2 * D + at + TILE]).astype(BF16)
        for sub in range(2):
            g = 2 * half + sub
            cut = slice(128 * sub, 128 * sub + 128)
            q_ref[g, :, 0:128] = qn[:, cut]
            for h in range(GROUP):
                mine = own_head == h
                rows = slice(h * TOK, h * TOK + TOK)
                k_ref[g, rows, 0:128] = jnp.where(mine, kn[:, cut], jnp.zeros((), BF16))
                v_ref[g, rows, 0:128] = jnp.where(mine, vb[:, cut], jnp.zeros((), BF16))


def lane_scales(scale_ref, g):
    out = jnp.zeros((1, SPAN), F32)
    for h in range(GROUP):
        out = jnp.where(iota((1, SPAN), 1) // TOK == h, scale_ref[g * GROUP + h] * LOG2E, out)
    return out


def attend(q_ref, k_ref, v_ref, scale_ref, att_ref, between):
    lane = iota((1, 128), 1)
    for g in range(HEADS // GROUP):
        shifted = q_ref[g, :, 128:256]
        for h in range(GROUP):
            score = dot(q_ref[g], k_ref[g, h * TOK : h * TOK + TOK, :], NT)
            peak = jnp.max(score, axis=-1, keepdims=True)
            shifted = jnp.where(lane == h * HEAD + 12, -peak.astype(BF16), shifted)
        q_ref[g, :, 128:256] = shifted
        scales = lane_scales(scale_ref, g)
        acc = None
        for j in range(SPAN // TILE):
            at = slice(TILE * j, TILE * j + TILE)
            powers = jnp.exp2(dot(q_ref[g], k_ref[g, at, :], NT) * scales[:, at]).astype(BF16)
            part = dot(powers, v_ref[g, at, :])
            acc = part if acc is None else acc + part
        att_ref[:, 128 * g : 128 * g + 128] = (acc[:, :128] / acc[:, 128:]).astype(BF16)
        between(g)


def ring_hop(own, gathered, way, step, send_sem, recv_sem):
    tall, wide, n_tall = lax.axis_index("tall"), lax.axis_index("wide"), lax.axis_size("tall")
    owner = lax.rem(tall + n_tall + (1 - step if way == 0 else step - 1), n_tall)
    return pltpu.make_async_remote_copy(
        src_ref=own if step == 1 else gathered.at[owner],
        dst_ref=gathered.at[owner],
        send_sem=send_sem.at[way, step - 1],
        recv_sem=recv_sem.at[way, step - 1],
        device_id=(wide, lax.rem(tall + (1 if way == 0 else n_tall - 1), n_tall)),
        device_id_type=MESH,
    )


def rem(a, n):
    return lax.rem(a, jnp.int32(n))


def div(a, n):
    return lax.div(a, jnp.int32(n))


def partner(k, sign):
    wide = lax.axis_index("wide")
    core, x, y = rem(wide, 2), rem(div(wide, 2), 4), div(wide, 8)
    turn = rem(64 - k, 64)
    step = rem(turn, 8)
    size = div(step + 1, 2)
    dy = size + rem(step + 1, 2) * (8 - 2 * size)
    dx, dc = rem(div(turn, 8), 4), div(turn, 32)
    return (rem(y + 8 + sign * dy, 8) * 4 + rem(x + 4 + sign * dx, 4)) * 2 + rem(core + 2 + sign * dc, 2)


def place_of(expert):
    wide = lax.axis_index("wide")
    dc = (expert % 2 + 2 - wide % 2) % 2
    dx = (expert // 2 % 4 + 4 - wide // 2 % 4) % 4
    dy = (expert // 8 + 8 - wide // 8) % 8
    step = jnp.where(dy == 0, 0, jnp.where(dy <= 4, 2 * dy - 1, 16 - 2 * dy))
    return (64 - (dc * 32 + dx * 8 + step)) % 64


def block_kernel(
    limits, experts,
    tokens_hbm, qkv_hbm, proj_hbm, attn_gain_ref, scale_ref, router_ref, in_hbm, out_hbm, moe_gain_ref, ids_ref, keep_ref,
    result_ref,
    tokens_ref, send, recv, qkv_ref, proj_ref, q_ref, k_ref, v_ref, att_ref, x_ref, x1_ref,
    scatter, gather, slots, arrived, made, back, hidden, gate, picked, w_in, w_out,
    load_sem, own_sem, send_sem, recv_sem, in_send, in_recv, out_send, out_recv, give_send, give_recv, take_send, take_recv,
):
    tall, wide = lax.axis_index("tall"), lax.axis_index("wide")
    n_tall, n_wide = lax.axis_size("tall"), lax.axis_size("wide")
    last = n_tall // 2
    loads = [
        pltpu.make_async_copy(tokens_hbm, tokens_ref, load_sem.at[0]),
        pltpu.make_async_copy(qkv_hbm, qkv_ref, load_sem.at[1]),
        pltpu.make_async_copy(proj_hbm, proj_ref, load_sem.at[2]),
        pltpu.make_async_copy(in_hbm, w_in.at[tall], load_sem.at[3]),
        pltpu.make_async_copy(out_hbm, w_out.at[tall], load_sem.at[4]),
    ]
    for load in loads:
        load.start()

    up, left = lax.rem(tall + n_tall - 1, n_tall), lax.rem(wide + n_wide - 1, n_wide)
    down, right = lax.rem(tall + 1, n_tall), lax.rem(wide + 1, n_wide)
    barrier = pltpu.get_barrier_semaphore()
    for peer in ((wide, up), (wide, down), (left, up), (right, down)):
        pl.semaphore_signal(barrier, inc=1, device_id=peer, device_id_type=MESH)

    def greet(k, carry):
        pl.semaphore_signal(barrier, inc=1, device_id=(rem(wide + k, n_wide), tall), device_id_type=MESH)
        return carry

    lax.fori_loop(1, n_wide, greet, 0)

    place = iota((TOK, TOK), 0)
    quad, rest = place // QUAD, place % QUAD
    row = rest // HALF + jnp.where(quad % 2 == 0, HALF, 0)
    col = rest % HALF + jnp.where(quad < 2, HALF, 0)
    pick = (iota((TOK, TOK), 1) == row * EDGE + col).astype(BF16)
    loads[0].wait()
    send[...] = dot(pick, tokens_ref[...]).astype(BF16)
    recv[0:QUAD, :] = send[0:QUAD, :]
    pl.semaphore_wait(barrier, n_wide + 3)
    copies = []
    for i, peer in enumerate([(wide, up), (left, tall), (left, up)]):
        rows = pl.ds(QUAD * (i + 1), QUAD)
        copies.append(
            pltpu.make_async_remote_copy(
                src_ref=send.at[rows], dst_ref=recv.at[rows], send_sem=send_sem.at[i], recv_sem=recv_sem.at[i],
                device_id=peer, device_id_type=MESH,
            )
        )
        copies[-1].start()

    hops = {}

    def launch(way, step):
        started = []
        if step < last or way == 0:
            started.append(ring_hop(in_hbm, w_in, way, step, in_send, in_recv))
        if step < last:
            started.append(ring_hop(out_hbm, w_out, way, step, out_send, out_recv))
        else:
            owner = lax.rem(tall + (n_tall + 1 - last if way == 0 else last - 1), n_tall)
            rows = pl.ds(TILE // 2 * way, TILE // 2)
            started.append(
                pltpu.make_async_remote_copy(
                    src_ref=w_out.at[owner, rows], dst_ref=w_out.at[owner, rows], send_sem=out_send.at[way, last - 1],
                    recv_sem=out_recv.at[way, last - 1], device_id=(wide, down if way == 0 else up),
                    device_id_type=MESH,
                )
            )
        for copy in started:
            copy.start()
        hops[way, step] = started

    def arrive(way, step):
        for copy in hops[way, step]:
            copy.wait_recv()

    def onward(way, step):
        arrive(way, step)
        launch(way, step + 1)

    launch(0, 1)

    per = 8
    groups = n_wide // per
    room = per * ROOM
    span = 2 * room
    ids, kept = ids_ref[...], keep_ref[...] == 1
    named = iota((experts, TOK), 0) == ids
    live = jnp.where(jnp.logical_and(named, kept), 1.0, 0.0)
    earlier = (iota((TOK, TOK), 0) < iota((TOK, TOK), 1)).astype(BF16)
    slot = jnp.sum(jnp.where(named, dot(live.astype(BF16), earlier), 0.0), axis=0, keepdims=True)
    target = jnp.where(kept, place_of(ids) * ROOM + slot.astype(I32), -1)
    scatter[...] = (iota((experts * ROOM, TOK), 0) == target).astype(BF16)
    eye = (iota((experts, experts), 0) == iota((experts, experts), 1)).astype(BF16)
    chosen = dot(live.astype(BF16), eye, TN)
    slot = jnp.sum(dot((live * slot).astype(BF16), eye, TN), axis=-1, keepdims=True)
    block = jnp.sum(chosen * place_of(iota((1, experts), 1)).astype(F32), axis=-1, keepdims=True)
    in_use = jnp.sum(chosen, axis=-1, keepdims=True)
    landing = jnp.where(in_use > 0.5, block * ROOM + slot, -1.0).astype(I32)
    for pair in range(groups // 2):
        gather[pair] = (iota((TOK, span), 1) + pair * span == landing).astype(BF16)

    features(scale_ref, region_column(*limits), q_ref, k_ref, v_ref)
    row, col = place // EDGE, place % EDGE
    quad = (row // HALF) + 2 * (col // HALF)
    pick = (iota((TOK, TOK), 1) == quad * QUAD + (row % HALF) * HALF + col % HALF).astype(BF16)
    for load in loads[1:]:
        load.wait()
    for copy in copies:
        copy.wait()
    launch(1, 1)
    x = dot(pick, recv[...]).astype(BF16)
    x_ref[...] = x
    prepare(x, qkv_ref, q_ref, k_ref, v_ref)

    def between(g):
        if g == 1:
            onward(0, 1)
        if g == 3:
            onward(1, 1)

    attend(q_ref, k_ref, v_ref, scale_ref, att_ref, between)
    out = dot(att_ref[...], proj_ref[...])
    x1_ref[...] = (x_ref[...].astype(F32) + norm(out, attn_gain_ref[...])).astype(BF16)

    def exchange(source, landing, send_sem, recv_sem, sign, group):
        def one(k, carry):
            rows = pl.ds(k * ROOM, ROOM)
            pltpu.make_async_remote_copy(
                src_ref=source.at[rows], dst_ref=landing.at[rows], send_sem=send_sem, recv_sem=recv_sem.at[group],
                device_id=(partner(k, sign), tall), device_id_type=MESH,
            ).start()
            return carry

        lax.fori_loop(max(1, group * per), group * per + per, one, 0)

    def whole_of(ref, blocks, send_sem, recv_sem):
        rows = pl.ds(0, blocks * ROOM)
        return pltpu.make_async_remote_copy(
            src_ref=ref.at[rows], dst_ref=ref.at[rows], send_sem=send_sem, recv_sem=recv_sem,
            device_id=(wide, down), device_id_type=MESH,
        )

    for pair in range(groups // 2):
        rows = slice(pair * span, pair * span + span)
        slots[rows] = dot(scatter[rows, :], x1_ref[...]).astype(BF16).reshape(span, WAYS, LANES)
        for group in (2 * pair, 2 * pair + 1):
            exchange(slots, arrived, give_send.at[0], give_recv, 1, group)
    arrived[0:ROOM] = slots[0:ROOM]
    onward(0, 2)
    logit = jnp.sum(dot(x1_ref[...], router_ref[...], NT) * chosen, axis=-1, keepdims=True)
    gate[...] = jnp.broadcast_to(in_use * jax.nn.sigmoid(logit), gate.shape)
    onward(1, 2)
    onward(0, 3)
    onward(1, 3)
    arrive(0, last)
    arrive(1, last)
    for group in range(groups):
        rows = slice(group * room, group * room + room)
        whole_of(arrived, per - (group == 0), give_send.at[0], give_recv.at[group]).wait_recv()
        here = arrived[rows].reshape(room, D)
        for c in range(n_tall):
            hidden[:, c * TILE : c * TILE + TILE] = gelu(dot(here, w_in[c])).astype(BF16)
        out = dot(hidden[...], w_out[...].reshape(n_tall * TILE, D)).astype(BF16)
        made[rows] = out.reshape(room, WAYS, LANES)
        exchange(made, back, take_send.at[0], take_recv, -1, group)
    back[0:ROOM] = made[0:ROOM]
    for started in hops.values():
        for copy in started:
            copy.wait_send()
    whole_of(slots, n_wide - 1, give_send.at[0], give_recv.at[0]).wait_send()
    for pair in range(groups // 2):
        for group in (2 * pair, 2 * pair + 1):
            whole_of(back, per - (group == 0), take_send.at[0], take_recv.at[group]).wait_recv()
        part = dot(gather[pair], back[pair * span : pair * span + span].reshape(span, D))
        if pair < groups // 2 - 1:
            picked[...] = part if pair == 0 else picked[...] + part
    result_ref[...] = (
        x1_ref[...].astype(F32) + gate[:, 0:1] * norm(picked[...] + part, moe_gain_ref[...])
    ).astype(BF16)
    whole_of(made, n_wide - 1, take_send.at[0], take_recv.at[0]).wait_send()


def body(
    tokens, qkv_weight, proj_weight, head_scale, attn_gain, router, expert_in, expert_out, moe_gain, expert_ids, keep
):
    n_tall, n_wide = lax.axis_size("tall"), lax.axis_size("wide")
    experts = router.shape[1]
    limits = (EDGE * n_tall, EDGE * n_wide)
    hidden = expert_in.shape[2]
    rows = pltpu.VMEM((TOK, D), BF16)
    slot_buffer = pltpu.VMEM((experts * ROOM, WAYS, LANES), BF16)
    DMA = pltpu.SemaphoreType.DMA
    ring_sem = DMA((2, n_tall // 2))
    out = pl.pallas_call(
        functools.partial(block_kernel, limits, experts),
        out_shape=jax.ShapeDtypeStruct((TOK, D), BF16),
        in_specs=[HBM, HBM, HBM, VMEM, SMEM, VMEM, HBM, HBM, VMEM, VMEM, VMEM],
        out_specs=VMEM,
        scratch_shapes=[
            rows, rows, rows,
            pltpu.VMEM((D, 3 * D), BF16),
            pltpu.VMEM((D, D), BF16),
            pltpu.VMEM((HEADS // GROUP, TOK, TILE), BF16),
            pltpu.VMEM((HEADS // GROUP, SPAN, TILE), BF16),
            pltpu.VMEM((HEADS // GROUP, SPAN, TILE), BF16),
            rows, rows, rows,
            pltpu.VMEM((experts * ROOM, TOK), BF16),
            pltpu.VMEM((4, TOK, experts * ROOM // 4), BF16),
            slot_buffer, slot_buffer, slot_buffer, slot_buffer,
            pltpu.VMEM((experts * ROOM // 8, n_tall * hidden), BF16),
            pltpu.VMEM((TOK, 128), F32),
            pltpu.VMEM((TOK, D), F32),
            pltpu.VMEM((n_tall, D, hidden), BF16),
            pltpu.VMEM((n_tall, hidden, D), BF16),
            DMA((5,)), DMA((1,)), DMA((3,)), DMA((3,)), ring_sem, ring_sem, ring_sem, ring_sem,
            DMA((1,)), DMA((8,)), DMA((1,)), DMA((8,)),
        ],
        compiler_params=pltpu.CompilerParams(collective_id=0, has_side_effects=True, vmem_limit_bytes=62 << 20),
        name="block",
    )(
        tokens.reshape(TOK, D), qkv_weight, proj_weight, attn_gain.reshape(1, D), head_scale, router.T, expert_in[0],
        expert_out[0], moe_gain.reshape(1, D), expert_ids.reshape(1, TOK), keep.reshape(1, TOK),
    )
    return out.reshape(EDGE, EDGE, D)


def solution(mesh):
    placed = (
        P("tall", "wide", None), P(), P(), P(), P(), P(), P("wide", None, "tall"), P("wide", "tall", None), P(),
        P("tall", "wide", None, None), P("tall", "wide", None),
    )
    return jax.shard_map(
        body, mesh=mesh, in_specs=placed, out_specs=P("tall", "wide", None), check_vma=False
    )
```

```python
import functools
import math

import jax
import jax.numpy as jnp
from jax import lax
from jax.experimental import pallas as pl
from jax.experimental.pallas import tpu as pltpu
from jax.sharding import PartitionSpec as P

F32, BF16, I32 = jnp.float32, jnp.bfloat16, jnp.int32
MESH = pl.DeviceIdType.MESH
EDGE = 24
HALF = EDGE // 2
TOK = EDGE * EDGE
QUAD = HALF * HALF
HEADS = 16
HEAD = 32
D = 512
GROUP = 4
SPAN = GROUP * TOK
TILE = 256
LOG2E = math.log2(math.e)
ROOM = 13
LANES = 128
TRIPLE = 3
THIRD = TOK // TRIPLE
WAYS = D // LANES
NT = (((1,), (1,)), ((), ()))
TN = (((0,), (0,)), ((), ()))
VMEM = pl.BlockSpec(memory_space=pltpu.VMEM)
SMEM = pl.BlockSpec(memory_space=pltpu.SMEM)
HBM = pl.BlockSpec(memory_space=pltpu.HBM)


def dot(a, b, dims=None):
    if dims is None:
        return jnp.dot(a, b, preferred_element_type=F32)
    return lax.dot_general(a, b, dims, preferred_element_type=F32)


def iota(shape, axis):
    return lax.broadcasted_iota(I32, shape, axis)


def norm(value, gain):
    mean = jnp.mean(value, axis=-1, keepdims=True)
    centred = value - mean
    return centred * lax.rsqrt(jnp.mean(centred * centred, axis=-1, keepdims=True) + 1e-5) * gain


def gelu(value):
    return 0.5 * value * (1.0 + lax.erf(value * math.sqrt(0.5)))


def unit(block):
    ones = (iota((TILE, TILE), 0) // HEAD == iota((TILE, TILE), 1) // HEAD).astype(BF16)
    square = block * block
    high = square.astype(BF16)
    low = (square - high.astype(F32)).astype(BF16)
    return (block * lax.rsqrt(dot(high, ones) + dot(low, ones) + 1e-6)).astype(BF16)


def region_column(total_rows, total_cols, stride=1):
    place = iota((TOK // stride, 1), 0) * stride
    row = lax.axis_index("tall") * EDGE + place // EDGE
    col = lax.axis_index("wide") * EDGE + place % EDGE
    return (row + HALF >= total_rows).astype(I32) * 2 + (col + HALF >= total_cols).astype(I32)


def features(scale_ref, region, region3, q_ref, k_ref, k3_ref, v_ref):
    lane = iota((1, 128), 1)
    feat, own_head = lane % HEAD, lane // HEAD
    key_feat = jnp.where(feat < 12, jnp.where(region == feat % 4, 0.0, -1.0), jnp.where(feat == 12, 1.0, 0.0))
    key3_feat = jnp.where(jnp.logical_and(feat < 12, region3 != feat % 4), -1.0, 0.0)
    for g in range(HEADS // GROUP):
        scale = jnp.ones((1, 128), F32)
        for h in range(GROUP):
            scale = jnp.where(own_head == h, scale_ref[g * GROUP + h], scale)
        whole = 100.0 / scale
        high = whole.astype(BF16).astype(F32)
        middle = (whole - high).astype(BF16).astype(F32)
        piece = jnp.where(feat < 4, high, jnp.where(feat < 8, middle, whole - high - middle))
        query_feat = jnp.where(jnp.logical_and(feat < 12, region == feat % 4), piece, 0.0)
        q_ref[g, :, 128:256] = query_feat.astype(BF16)
        for h in range(GROUP):
            mine = own_head == h
            rows = slice(h * TOK, h * TOK + TOK)
            k_ref[g, rows, 128:256] = jnp.where(mine, key_feat, 0.0).astype(BF16)
            k3_ref[g, h * THIRD : h * THIRD + THIRD, 128:256] = jnp.where(mine, key3_feat, 0.0).astype(BF16)
            v_ref[g, rows, 128:256] = jnp.broadcast_to(jnp.where(mine, 1.0, 0.0), (TOK, 128)).astype(BF16)


def prepare(x, qkv_ref, q_ref, k_ref, k3_ref, v_ref):
    own_head = iota((1, 128), 1) // HEAD
    thirds = (iota((THIRD, TOK), 1) // TRIPLE == iota((THIRD, TOK), 0)).astype(BF16)
    for half in range(2):
        at = TILE * half
        qn = unit(dot(x, qkv_ref[:, at : at + TILE]))
        kn = unit(dot(x, qkv_ref[:, D + at : D + at + TILE]))
        k3 = (dot(thirds, kn) * (1.0 / TRIPLE)).astype(BF16)
        vb = dot(x, qkv_ref[:, 2 * D + at : 2 * D + at + TILE]).astype(BF16)
        for sub in range(2):
            g = 2 * half + sub
            cut = slice(128 * sub, 128 * sub + 128)
            q_ref[g, :, 0:128] = qn[:, cut]
            for h in range(GROUP):
                mine = own_head == h
                rows = slice(h * TOK, h * TOK + TOK)
                k_ref[g, rows, 0:128] = jnp.where(mine, kn[:, cut], jnp.zeros((), BF16))
                k3_ref[g, h * THIRD : h * THIRD + THIRD, 0:128] = jnp.where(mine, k3[:, cut], jnp.zeros((), BF16))
                v_ref[g, rows, 0:128] = jnp.where(mine, vb[:, cut], jnp.zeros((), BF16))


def lane_scales(scale_ref, g):
    out = jnp.zeros((1, SPAN), F32)
    for h in range(GROUP):
        out = jnp.where(iota((1, SPAN), 1) // TOK == h, scale_ref[g * GROUP + h] * LOG2E, out)
    return out


def attend(q_ref, k_ref, k3_ref, v_ref, scale_ref, att_ref, between):
    lane = iota((1, 128), 1)
    for g in range(HEADS // GROUP):
        shifted = q_ref[g, :, 128:256]
        score = dot(q_ref[g], k3_ref[g], NT)
        tops = [None] * GROUP
        for n in range(GROUP * THIRD // 128):
            piece = score[:, 128 * n : 128 * n + 128]
            low, high = 128 * n // THIRD, (128 * n + 127) // THIRD
            edge = high * THIRD - 128 * n
            for h in range(low, high + 1):
                part = piece
                if low != high:
                    part = jnp.where((lane < edge) if h == low else (lane >= edge), piece, -jnp.inf)
                tops[h] = part if tops[h] is None else jnp.maximum(tops[h], part)
        for h in range(GROUP):
            shift = -(jnp.max(tops[h], axis=-1, keepdims=True) + 2.0 / 3.0)
            shifted = jnp.where(lane == h * HEAD + 12, shift.astype(BF16), shifted)
        q_ref[g, :, 128:256] = shifted
        scales = lane_scales(scale_ref, g)
        acc = None
        for j in range(SPAN // TILE):
            at = slice(TILE * j, TILE * j + TILE)
            powers = jnp.exp2(dot(q_ref[g], k_ref[g, at, :], NT) * scales[:, at]).astype(BF16)
            part = dot(powers, v_ref[g, at, :])
            acc = part if acc is None else acc + part
        att_ref[:, 128 * g : 128 * g + 128] = (acc[:, :128] / acc[:, 128:]).astype(BF16)
        between(g)


def ring_hop(own, gathered, way, step, send_sem, recv_sem):
    tall, wide, n_tall = lax.axis_index("tall"), lax.axis_index("wide"), lax.axis_size("tall")
    owner = lax.rem(tall + n_tall + (1 - step if way == 0 else step - 1), n_tall)
    return pltpu.make_async_remote_copy(
        src_ref=own if step == 1 else gathered.at[owner],
        dst_ref=gathered.at[owner],
        send_sem=send_sem.at[way, step - 1],
        recv_sem=recv_sem.at[way, step - 1],
        device_id=(wide, lax.rem(tall + (1 if way == 0 else n_tall - 1), n_tall)),
        device_id_type=MESH,
    )


def rem(a, n):
    return lax.rem(a, jnp.int32(n))


def div(a, n):
    return lax.div(a, jnp.int32(n))


def partner(k, sign):
    wide = lax.axis_index("wide")
    core, x, y = rem(wide, 2), rem(div(wide, 2), 4), div(wide, 8)
    turn = rem(64 - k, 64)
    step = rem(turn, 8)
    size = div(step + 1, 2)
    dy = size + rem(step + 1, 2) * (8 - 2 * size)
    dx, dc = rem(div(turn, 8), 4), div(turn, 32)
    return (rem(y + 8 + sign * dy, 8) * 4 + rem(x + 4 + sign * dx, 4)) * 2 + rem(core + 2 + sign * dc, 2)


def place_of(expert):
    wide = lax.axis_index("wide")
    dc = (expert % 2 + 2 - wide % 2) % 2
    dx = (expert // 2 % 4 + 4 - wide // 2 % 4) % 4
    dy = (expert // 8 + 8 - wide // 8) % 8
    step = jnp.where(dy == 0, 0, jnp.where(dy <= 4, 2 * dy - 1, 16 - 2 * dy))
    return (64 - (dc * 32 + dx * 8 + step)) % 64


def block_kernel(
    limits, experts,
    tokens_hbm, qkv_hbm, proj_hbm, attn_gain_ref, scale_ref, router_ref, in_hbm, out_hbm, moe_gain_ref, ids_ref, keep_ref,
    result_ref,
    tokens_ref, send, recv, qkv_ref, proj_ref, q_ref, k_ref, k3_ref, v_ref, att_ref, x_ref, x1_ref,
    scatter, gather, slots, arrived, made, back, hidden, gate, picked, w_in, w_out,
    load_sem, line_sem, send_sem, recv_sem, in_send, in_recv, out_send, out_recv, give_send, give_recv, take_send, take_recv,
):
    tall, wide = lax.axis_index("tall"), lax.axis_index("wide")
    n_tall, n_wide = lax.axis_size("tall"), lax.axis_size("wide")
    last = n_tall // 2
    loads = [
        pltpu.make_async_copy(tokens_hbm, tokens_ref, load_sem.at[0]),
        pltpu.make_async_copy(qkv_hbm, qkv_ref, load_sem.at[1]),
        pltpu.make_async_copy(proj_hbm, proj_ref, load_sem.at[2]),
        pltpu.make_async_copy(in_hbm, w_in.at[tall], load_sem.at[3]),
        pltpu.make_async_copy(out_hbm, w_out.at[tall], load_sem.at[4]),
    ]
    for load in loads:
        load.start()

    up, left = lax.rem(tall + n_tall - 1, n_tall), lax.rem(wide + n_wide - 1, n_wide)
    down, right = lax.rem(tall + 1, n_tall), lax.rem(wide + 1, n_wide)
    barrier = pltpu.get_barrier_semaphore()
    near = [(wide, up), (wide, down), (left, up), (right, down), (left, tall), (right, tall)]
    row_start, row_place = div(wide, 8) * 8, rem(wide, 8)
    across = [(rem(wide + 8 * i, n_wide), tall) for i in range(1, 8)]
    near += across + [(row_start + rem(row_place + i, 8), tall) for i in range(1, 8)]
    for peer in near:
        pl.semaphore_signal(barrier, inc=1, device_id=peer, device_id_type=MESH)

    place = iota((TOK, TOK), 0)
    quad, rest = place // QUAD, place % QUAD
    row = rest // HALF + jnp.where(quad % 2 == 0, HALF, 0)
    col = rest % HALF + jnp.where(quad < 2, HALF, 0)
    pick = (iota((TOK, TOK), 1) == row * EDGE + col).astype(BF16)
    loads[0].wait()
    send[...] = dot(pick, tokens_ref[...]).astype(BF16)
    recv[0:QUAD, :] = send[0:QUAD, :]
    pl.semaphore_wait(barrier, len(near))
    copies = []
    for i, peer in enumerate([(wide, up), (left, tall), (left, up)]):
        rows = pl.ds(QUAD * (i + 1), QUAD)
        copies.append(
            pltpu.make_async_remote_copy(
                src_ref=send.at[rows], dst_ref=recv.at[rows], send_sem=send_sem.at[i], recv_sem=recv_sem.at[i],
                device_id=peer, device_id_type=MESH,
            )
        )
        copies[-1].start()

    hops = {}

    def launch(kind, way, step):
        if step < last or (kind == 0 and way == 0):
            if kind == 0:
                copy = ring_hop(in_hbm, w_in, way, step, in_send, in_recv)
            else:
                copy = ring_hop(out_hbm, w_out, way, step, out_send, out_recv)
        else:
            owner = lax.rem(tall + (n_tall + 1 - last if way == 0 else last - 1), n_tall)
            rows = pl.ds(TILE // 2 * way, TILE // 2)
            copy = pltpu.make_async_remote_copy(
                src_ref=w_out.at[owner, rows], dst_ref=w_out.at[owner, rows], send_sem=out_send.at[way, last - 1],
                recv_sem=out_recv.at[way, last - 1], device_id=(wide, down if way == 0 else up), device_id_type=MESH,
            )
        copy.start()
        hops[kind, way, step] = copy

    def onward(kind, way, step):
        hops[kind, way, step].wait_recv()
        launch(kind, way, step + 1)

    launch(0, 0, 1)
    for peer in across:
        pl.semaphore_signal(line_sem, inc=1, device_id=peer, device_id_type=MESH)

    per = 8
    groups = n_wide // per
    room = per * ROOM
    span = 2 * room
    ids, kept = ids_ref[...], keep_ref[...] == 1
    named = iota((experts, TOK), 0) == ids
    live = jnp.where(jnp.logical_and(named, kept), 1.0, 0.0)
    earlier = (iota((TOK, TOK), 0) < iota((TOK, TOK), 1)).astype(BF16)
    slot = jnp.sum(jnp.where(named, dot(live.astype(BF16), earlier), 0.0), axis=0, keepdims=True)
    target = jnp.where(kept, place_of(ids) * ROOM + slot.astype(I32), -1)
    scatter[...] = (iota((experts * ROOM, TOK), 0) == target).astype(BF16)
    eye = (iota((experts, experts), 0) == iota((experts, experts), 1)).astype(BF16)
    chosen = dot(live.astype(BF16), eye, TN)
    slot = jnp.sum(dot((live * slot).astype(BF16), eye, TN), axis=-1, keepdims=True)
    block = jnp.sum(chosen * place_of(iota((1, experts), 1)).astype(F32), axis=-1, keepdims=True)
    in_use = jnp.sum(chosen, axis=-1, keepdims=True)
    landing = jnp.where(in_use > 0.5, block * ROOM + slot, -1.0).astype(I32)
    for pair in range(groups // 2):
        gather[pair] = (iota((TOK, span), 1) + pair * span == landing).astype(BF16)

    launch(1, 0, 1)
    features(scale_ref, region_column(*limits), region_column(*limits, TRIPLE), q_ref, k_ref, k3_ref, v_ref)
    row, col = place // EDGE, place % EDGE
    quad = (row // HALF) + 2 * (col // HALF)
    pick = (iota((TOK, TOK), 1) == quad * QUAD + (row % HALF) * HALF + col % HALF).astype(BF16)
    for load in loads[1:]:
        load.wait()
    for copy in copies:
        copy.wait()
    launch(0, 1, 1)
    x = dot(pick, recv[...]).astype(BF16)
    x_ref[...] = x
    prepare(x, qkv_ref, q_ref, k_ref, k3_ref, v_ref)
    launch(1, 1, 1)

    def between(g):
        for kind, way, step in (((0, 0, 1),), ((1, 0, 1),), ((0, 1, 1),), ((1, 1, 1), (0, 0, 2)))[g]:
            onward(kind, way, step)

    attend(q_ref, k_ref, k3_ref, v_ref, scale_ref, att_ref, between)
    out = dot(att_ref[...], proj_ref[...])
    x1_ref[...] = (x_ref[...].astype(F32) + norm(out, attn_gain_ref[...])).astype(BF16)
    pl.semaphore_wait(line_sem, len(across))

    def exchange(source, landing, send_sem, recv_sem, sign, group):
        def one(k, carry):
            rows = pl.ds(k * ROOM, ROOM)
            pltpu.make_async_remote_copy(
                src_ref=source.at[rows], dst_ref=landing.at[rows], send_sem=send_sem, recv_sem=recv_sem.at[group],
                device_id=(partner(k, sign), tall), device_id_type=MESH,
            ).start()
            return carry

        lax.fori_loop(max(1, group * per), group * per + per, one, 0)

    def whole_of(ref, blocks, send_sem, recv_sem):
        rows = pl.ds(0, blocks * ROOM)
        return pltpu.make_async_remote_copy(
            src_ref=ref.at[rows], dst_ref=ref.at[rows], send_sem=send_sem, recv_sem=recv_sem,
            device_id=(wide, down), device_id_type=MESH,
        )

    for pair in range(groups // 2):
        rows = slice(pair * span, pair * span + span)
        slots[rows] = dot(scatter[rows, :], x1_ref[...]).astype(BF16).reshape(span, WAYS, LANES)
        for group in (2 * pair, 2 * pair + 1):
            exchange(slots, arrived, give_send.at[0], give_recv, 1, group)
        if pair > 0:
            onward(*((1, 0, 2), (0, 1, 2), (1, 1, 2))[pair - 1])
    arrived[0:ROOM] = slots[0:ROOM]
    logit = jnp.sum(dot(x1_ref[...], router_ref[...], NT) * chosen, axis=-1, keepdims=True)
    gate[...] = jnp.broadcast_to(in_use * jax.nn.sigmoid(logit), gate.shape)
    onward(0, 0, 3)
    onward(1, 0, 3)
    hops[0, 1, 3].wait_recv()
    onward(1, 1, 3)
    hops[0, 0, last].wait_recv()
    for group in range(groups):
        rows = slice(group * room, group * room + room)
        whole_of(arrived, per - (group == 0), give_send.at[0], give_recv.at[group]).wait_recv()
        here = arrived[rows].reshape(room, D)
        for c in range(n_tall):
            hidden[:, c * TILE : c * TILE + TILE] = gelu(dot(here, w_in[c])).astype(BF16)
        if group == 0:
            hops[1, 0, last].wait_recv()
            hops[1, 1, last].wait_recv()
        out = dot(hidden[...], w_out[...].reshape(n_tall * TILE, D)).astype(BF16)
        made[rows] = out.reshape(room, WAYS, LANES)
        exchange(made, back, take_send.at[0], take_recv, -1, group)
    back[0:ROOM] = made[0:ROOM]
    for copy in hops.values():
        copy.wait_send()
    whole_of(slots, n_wide - 1, give_send.at[0], give_recv.at[0]).wait_send()
    for pair in range(groups // 2):
        for group in (2 * pair, 2 * pair + 1):
            whole_of(back, per - (group == 0), take_send.at[0], take_recv.at[group]).wait_recv()
        part = dot(gather[pair], back[pair * span : pair * span + span].reshape(span, D))
        if pair < groups // 2 - 1:
            picked[...] = part if pair == 0 else picked[...] + part
    result_ref[...] = (
        x1_ref[...].astype(F32) + gate[:, 0:1] * norm(picked[...] + part, moe_gain_ref[...])
    ).astype(BF16)
    whole_of(made, n_wide - 1, take_send.at[0], take_recv.at[0]).wait_send()


def body(
    tokens, qkv_weight, proj_weight, head_scale, attn_gain, router, expert_in, expert_out, moe_gain, expert_ids, keep
):
    n_tall, n_wide = lax.axis_size("tall"), lax.axis_size("wide")
    experts = router.shape[1]
    limits = (EDGE * n_tall, EDGE * n_wide)
    hidden = expert_in.shape[2]
    rows = pltpu.VMEM((TOK, D), BF16)
    slot_buffer = pltpu.VMEM((experts * ROOM, WAYS, LANES), BF16)
    DMA = pltpu.SemaphoreType.DMA
    ring_sem = DMA((2, n_tall // 2))
    out = pl.pallas_call(
        functools.partial(block_kernel, limits, experts),
        out_shape=jax.ShapeDtypeStruct((TOK, D), BF16),
        in_specs=[HBM, HBM, HBM, VMEM, SMEM, VMEM, HBM, HBM, VMEM, VMEM, VMEM],
        out_specs=VMEM,
        scratch_shapes=[
            rows, rows, rows,
            pltpu.VMEM((D, 3 * D), BF16),
            pltpu.VMEM((D, D), BF16),
            pltpu.VMEM((HEADS // GROUP, TOK, TILE), BF16),
            pltpu.VMEM((HEADS // GROUP, SPAN, TILE), BF16),
            pltpu.VMEM((HEADS // GROUP, GROUP * THIRD, TILE), BF16),
            pltpu.VMEM((HEADS // GROUP, SPAN, TILE), BF16),
            rows, rows, rows,
            pltpu.VMEM((experts * ROOM, TOK), BF16),
            pltpu.VMEM((4, TOK, experts * ROOM // 4), BF16),
            slot_buffer, slot_buffer, slot_buffer, slot_buffer,
            pltpu.VMEM((experts * ROOM // 8, n_tall * hidden), BF16),
            pltpu.VMEM((TOK, 128), F32),
            pltpu.VMEM((TOK, D), F32),
            pltpu.VMEM((n_tall, D, hidden), BF16),
            pltpu.VMEM((n_tall, hidden, D), BF16),
            DMA((5,)), pltpu.SemaphoreType.REGULAR, DMA((3,)), DMA((3,)), ring_sem, ring_sem, ring_sem, ring_sem,
            DMA((1,)), DMA((8,)), DMA((1,)), DMA((8,)),
        ],
        compiler_params=pltpu.CompilerParams(collective_id=0, has_side_effects=True, vmem_limit_bytes=62 << 20),
        name="block",
    )(
        tokens.reshape(TOK, D), qkv_weight, proj_weight, attn_gain.reshape(1, D), head_scale, router.T, expert_in[0],
        expert_out[0], moe_gain.reshape(1, D), expert_ids.reshape(1, TOK), keep.reshape(1, TOK),
    )
    return out.reshape(EDGE, EDGE, D)


def solution(mesh):
    placed = (
        P("tall", "wide", None), P(), P(), P(), P(), P(), P("wide", None, "tall"), P("wide", "tall", None), P(),
        P("tall", "wide", None, None), P("tall", "wide", None),
    )
    return jax.shard_map(
        body, mesh=mesh, in_specs=placed, out_specs=P("tall", "wide", None), check_vma=False
    )
```

```python
import functools
import math

import jax
import jax.numpy as jnp
from jax import lax
from jax.experimental import pallas as pl
from jax.experimental.pallas import tpu as pltpu
from jax.sharding import PartitionSpec as P

F32, BF16, I32 = jnp.float32, jnp.bfloat16, jnp.int32
MESH = pl.DeviceIdType.MESH
EDGE = 24
HALF = EDGE // 2
TOK = EDGE * EDGE
QUAD = HALF * HALF
HEADS = 16
HEAD = 32
D = 512
GROUP = 4
SPAN = GROUP * TOK
TILE = 256
LOG2E = math.log2(math.e)
ROOM = 13
LANES = 128
TRIPLE = 3
THIRD = TOK // TRIPLE
WAYS = D // LANES
NT = (((1,), (1,)), ((), ()))
TN = (((0,), (0,)), ((), ()))
VMEM = pl.BlockSpec(memory_space=pltpu.VMEM)
SMEM = pl.BlockSpec(memory_space=pltpu.SMEM)
HBM = pl.BlockSpec(memory_space=pltpu.HBM)


def dot(a, b, dims=None):
    if dims is None:
        return jnp.dot(a, b, preferred_element_type=F32)
    return lax.dot_general(a, b, dims, preferred_element_type=F32)


def iota(shape, axis):
    return lax.broadcasted_iota(I32, shape, axis)


def norm(value, gain):
    mean = jnp.mean(value, axis=-1, keepdims=True)
    centred = value - mean
    return centred * lax.rsqrt(jnp.mean(centred * centred, axis=-1, keepdims=True) + 1e-5) * gain


def gelu(value):
    return 0.5 * value * (1.0 + lax.erf(value * math.sqrt(0.5)))


def unit(block):
    ones = (iota((TILE, TILE), 0) // HEAD == iota((TILE, TILE), 1) // HEAD).astype(BF16)
    square = block * block
    high = square.astype(BF16)
    low = (square - high.astype(F32)).astype(BF16)
    return (block * lax.rsqrt(dot(high, ones) + dot(low, ones) + 1e-6)).astype(BF16)


def region_column(total_rows, total_cols, stride=1):
    place = iota((TOK // stride, 1), 0) * stride
    row = lax.axis_index("tall") * EDGE + place // EDGE
    col = lax.axis_index("wide") * EDGE + place % EDGE
    return (row + HALF >= total_rows).astype(I32) * 2 + (col + HALF >= total_cols).astype(I32)


def features(scale_ref, region, region3, q_ref, k_ref, k3_ref, v_ref):
    lane = iota((1, 128), 1)
    feat, own_head = lane % HEAD, lane // HEAD
    key_feat = jnp.where(feat < 12, jnp.where(region == feat % 4, 0.0, -1.0), jnp.where(feat == 12, 1.0, 0.0))
    key3_feat = jnp.where(jnp.logical_and(feat < 12, region3 != feat % 4), -1.0, 0.0)
    for g in range(HEADS // GROUP):
        scale = jnp.ones((1, 128), F32)
        for h in range(GROUP):
            scale = jnp.where(own_head == h, scale_ref[g * GROUP + h], scale)
        whole = 100.0 / scale
        high = whole.astype(BF16).astype(F32)
        middle = (whole - high).astype(BF16).astype(F32)
        piece = jnp.where(feat < 4, high, jnp.where(feat < 8, middle, whole - high - middle))
        query_feat = jnp.where(jnp.logical_and(feat < 12, region == feat % 4), piece, 0.0)
        q_ref[g, :, 128:256] = query_feat.astype(BF16)
        for h in range(GROUP):
            mine = own_head == h
            rows = slice(h * TOK, h * TOK + TOK)
            k_ref[g, rows, 128:256] = jnp.where(mine, key_feat, 0.0).astype(BF16)
            k3_ref[g, h * THIRD : h * THIRD + THIRD, 128:256] = jnp.where(mine, key3_feat, 0.0).astype(BF16)
            v_ref[g, rows, 128:256] = jnp.broadcast_to(jnp.where(mine, 1.0, 0.0), (TOK, 128)).astype(BF16)


def prepare(x, qkv_ref, q_ref, k_ref, k3_ref, v_ref):
    own_head = iota((1, 128), 1) // HEAD
    thirds = (iota((THIRD, TOK), 1) // TRIPLE == iota((THIRD, TOK), 0)).astype(BF16)
    for half in range(2):
        at = TILE * half
        qn = unit(dot(x, qkv_ref[:, at : at + TILE]))
        kn = unit(dot(x, qkv_ref[:, D + at : D + at + TILE]))
        k3 = (dot(thirds, kn) * (1.0 / TRIPLE)).astype(BF16)
        vb = dot(x, qkv_ref[:, 2 * D + at : 2 * D + at + TILE]).astype(BF16)
        for sub in range(2):
            g = 2 * half + sub
            cut = slice(128 * sub, 128 * sub + 128)
            q_ref[g, :, 0:128] = qn[:, cut]
            for h in range(GROUP):
                mine = own_head == h
                rows = slice(h * TOK, h * TOK + TOK)
                k_ref[g, rows, 0:128] = jnp.where(mine, kn[:, cut], jnp.zeros((), BF16))
                k3_ref[g, h * THIRD : h * THIRD + THIRD, 0:128] = jnp.where(mine, k3[:, cut], jnp.zeros((), BF16))
                v_ref[g, rows, 0:128] = jnp.where(mine, vb[:, cut], jnp.zeros((), BF16))


def lane_scales(scale_ref, g):
    out = jnp.zeros((1, SPAN), F32)
    for h in range(GROUP):
        out = jnp.where(iota((1, SPAN), 1) // TOK == h, scale_ref[g * GROUP + h] * LOG2E, out)
    return out


def attend(q_ref, k_ref, k3_ref, v_ref, scale_ref, att_ref, between):
    lane = iota((1, 128), 1)
    for g in range(HEADS // GROUP):
        shifted = q_ref[g, :, 128:256]
        score = dot(q_ref[g], k3_ref[g], NT)
        tops = [None] * GROUP
        for n in range(GROUP * THIRD // 128):
            piece = score[:, 128 * n : 128 * n + 128]
            low, high = 128 * n // THIRD, (128 * n + 127) // THIRD
            edge = high * THIRD - 128 * n
            for h in range(low, high + 1):
                part = piece
                if low != high:
                    part = jnp.where((lane < edge) if h == low else (lane >= edge), piece, -jnp.inf)
                tops[h] = part if tops[h] is None else jnp.maximum(tops[h], part)
        for h in range(GROUP):
            shift = -(jnp.max(tops[h], axis=-1, keepdims=True) + 2.0 / 3.0)
            shifted = jnp.where(lane == h * HEAD + 12, shift.astype(BF16), shifted)
        q_ref[g, :, 128:256] = shifted
        scales = lane_scales(scale_ref, g)
        acc = None
        for j in range(SPAN // TILE):
            at = slice(TILE * j, TILE * j + TILE)
            powers = jnp.exp2(dot(q_ref[g], k_ref[g, at, :], NT) * scales[:, at]).astype(BF16)
            part = dot(powers, v_ref[g, at, :])
            acc = part if acc is None else acc + part
        att_ref[:, 128 * g : 128 * g + 128] = (acc[:, :128] / acc[:, 128:]).astype(BF16)
        between(g)


def ring_hop(own, gathered, way, step, send_sem, recv_sem):
    tall, wide, n_tall = lax.axis_index("tall"), lax.axis_index("wide"), lax.axis_size("tall")
    owner = lax.rem(tall + n_tall + (1 - step if way == 0 else step - 1), n_tall)
    return pltpu.make_async_remote_copy(
        src_ref=own if step == 1 else gathered.at[owner],
        dst_ref=gathered.at[owner],
        send_sem=send_sem.at[way, step - 1],
        recv_sem=recv_sem.at[way, step - 1],
        device_id=(wide, lax.rem(tall + (1 if way == 0 else n_tall - 1), n_tall)),
        device_id_type=MESH,
    )


def rem(a, n):
    return lax.rem(a, jnp.int32(n))


def div(a, n):
    return lax.div(a, jnp.int32(n))


def partner(k, sign):
    wide = lax.axis_index("wide")
    core, x, y = rem(wide, 2), rem(div(wide, 2), 4), div(wide, 8)
    turn = rem(64 - k, 64)
    step = rem(turn, 8)
    size = div(step + 1, 2)
    dy = size + rem(step + 1, 2) * (8 - 2 * size)
    dx, dc = rem(div(turn, 8), 4), div(turn, 32)
    return (rem(y + 8 + sign * dy, 8) * 4 + rem(x + 4 + sign * dx, 4)) * 2 + rem(core + 2 + sign * dc, 2)


def place_of(expert):
    wide = lax.axis_index("wide")
    dc = (expert % 2 + 2 - wide % 2) % 2
    dx = (expert // 2 % 4 + 4 - wide // 2 % 4) % 4
    dy = (expert // 8 + 8 - wide // 8) % 8
    step = jnp.where(dy == 0, 0, jnp.where(dy <= 4, 2 * dy - 1, 16 - 2 * dy))
    return (64 - (dc * 32 + dx * 8 + step)) % 64


def block_kernel(
    limits, experts,
    tokens_hbm, qkv_hbm, proj_hbm, attn_gain_ref, scale_ref, router_ref, in_hbm, out_hbm, moe_gain_ref, ids_ref, keep_ref,
    result_ref,
    tokens_ref, send, recv, qkv_ref, proj_ref, q_ref, k_ref, k3_ref, v_ref, att_ref, x_ref, x1_ref,
    scatter, gather, slots, arrived, made, back, hidden, gate, picked, w_in, w_out,
    load_sem, line_sem, send_sem, recv_sem, in_send, in_recv, out_send, out_recv, give_send, give_recv, take_send, take_recv,
):
    tall, wide = lax.axis_index("tall"), lax.axis_index("wide")
    n_tall, n_wide = lax.axis_size("tall"), lax.axis_size("wide")
    last = n_tall // 2
    loads = [
        pltpu.make_async_copy(tokens_hbm, tokens_ref, load_sem.at[0]),
        pltpu.make_async_copy(qkv_hbm, qkv_ref, load_sem.at[1]),
        pltpu.make_async_copy(proj_hbm, proj_ref, load_sem.at[2]),
        pltpu.make_async_copy(in_hbm, w_in.at[tall], load_sem.at[3]),
        pltpu.make_async_copy(out_hbm.at[:, pl.ds(0, TILE)], w_out.at[0, tall], load_sem.at[4]),
        pltpu.make_async_copy(out_hbm.at[:, pl.ds(TILE, TILE)], w_out.at[1, tall], load_sem.at[5]),
    ]
    for load in loads:
        load.start()

    up, left = lax.rem(tall + n_tall - 1, n_tall), lax.rem(wide + n_wide - 1, n_wide)
    down, right = lax.rem(tall + 1, n_tall), lax.rem(wide + 1, n_wide)
    barrier = pltpu.get_barrier_semaphore()
    near = [(wide, up), (wide, down), (left, up), (right, down), (left, tall), (right, tall)]
    row_start, row_place = div(wide, 8) * 8, rem(wide, 8)
    across = [(rem(wide + 8 * i, n_wide), tall) for i in range(1, 8)]
    near += across + [(row_start + rem(row_place + i, 8), tall) for i in range(1, 8)]
    for peer in near:
        pl.semaphore_signal(barrier, inc=1, device_id=peer, device_id_type=MESH)

    place = iota((TOK, TOK), 0)
    quad, rest = place // QUAD, place % QUAD
    row = rest // HALF + jnp.where(quad % 2 == 0, HALF, 0)
    col = rest % HALF + jnp.where(quad < 2, HALF, 0)
    pick = (iota((TOK, TOK), 1) == row * EDGE + col).astype(BF16)
    loads[0].wait()
    send[...] = dot(pick, tokens_ref[...]).astype(BF16)
    recv[0:QUAD, :] = send[0:QUAD, :]
    pl.semaphore_wait(barrier, len(near))
    copies = []
    for i, peer in enumerate([(wide, up), (left, tall), (left, up)]):
        rows = pl.ds(QUAD * (i + 1), QUAD)
        copies.append(
            pltpu.make_async_remote_copy(
                src_ref=send.at[rows], dst_ref=recv.at[rows], send_sem=send_sem.at[i], recv_sem=recv_sem.at[i],
                device_id=peer, device_id_type=MESH,
            )
        )
        copies[-1].start()

    hops = {}

    def launch(kind, way, step):
        if kind == 0:
            copy = ring_hop(in_hbm, w_in, way, step, in_send, in_recv)
        elif step < last:
            copy = ring_hop(
                out_hbm.at[:, pl.ds(TILE * (kind - 1), TILE)], w_out.at[kind - 1], way, step,
                out_send.at[kind - 1], out_recv.at[kind - 1],
            )
        else:
            owner = lax.rem(tall + (n_tall + 1 - last if way == 0 else last - 1), n_tall)
            block = w_out.at[kind - 1, owner, pl.ds(TILE // 2 * way, TILE // 2)]
            copy = pltpu.make_async_remote_copy(
                src_ref=block, dst_ref=block, send_sem=out_send.at[kind - 1, way, last - 1],
                recv_sem=out_recv.at[kind - 1, way, last - 1], device_id=(wide, down if way == 0 else up),
                device_id_type=MESH,
            )
        copy.start()
        hops[kind, way, step] = copy

    def onward(kind, way, step):
        hops[kind, way, step].wait_recv()
        launch(kind, way, step + 1)

    launch(0, 0, 1)
    for peer in across:
        pl.semaphore_signal(line_sem, inc=1, device_id=peer, device_id_type=MESH)

    per = 8
    groups = n_wide // per
    room = per * ROOM
    span = 2 * room
    ids, kept = ids_ref[...], keep_ref[...] == 1
    named = iota((experts, TOK), 0) == ids
    live = jnp.where(jnp.logical_and(named, kept), 1.0, 0.0)
    earlier = (iota((TOK, TOK), 0) < iota((TOK, TOK), 1)).astype(BF16)
    slot = jnp.sum(jnp.where(named, dot(live.astype(BF16), earlier), 0.0), axis=0, keepdims=True)
    target = jnp.where(kept, place_of(ids) * ROOM + slot.astype(I32), -1)
    scatter[...] = (iota((experts * ROOM, TOK), 0) == target).astype(BF16)
    eye = (iota((experts, experts), 0) == iota((experts, experts), 1)).astype(BF16)
    chosen = dot(live.astype(BF16), eye, TN)
    slot = jnp.sum(dot((live * slot).astype(BF16), eye, TN), axis=-1, keepdims=True)
    block = jnp.sum(chosen * place_of(iota((1, experts), 1)).astype(F32), axis=-1, keepdims=True)
    in_use = jnp.sum(chosen, axis=-1, keepdims=True)
    landing = jnp.where(in_use > 0.5, block * ROOM + slot, -1.0).astype(I32)
    for pair in range(groups // 2):
        gather[pair] = (iota((TOK, span), 1) + pair * span == landing).astype(BF16)

    launch(1, 0, 1)
    features(scale_ref, region_column(*limits), region_column(*limits, TRIPLE), q_ref, k_ref, k3_ref, v_ref)
    row, col = place // EDGE, place % EDGE
    quad = (row // HALF) + 2 * (col // HALF)
    pick = (iota((TOK, TOK), 1) == quad * QUAD + (row % HALF) * HALF + col % HALF).astype(BF16)
    for load in loads[1:]:
        load.wait()
    for copy in copies:
        copy.wait()
    launch(0, 1, 1)
    x = dot(pick, recv[...]).astype(BF16)
    x_ref[...] = x
    prepare(x, qkv_ref, q_ref, k_ref, k3_ref, v_ref)
    launch(1, 1, 1)

    def between(g):
        for kind, way, step in (((0, 0, 1),), ((1, 0, 1),), ((0, 1, 1),), ((1, 1, 1), (0, 0, 2)))[g]:
            onward(kind, way, step)
        if g % 2:
            launch(2, g // 2, 1)

    attend(q_ref, k_ref, k3_ref, v_ref, scale_ref, att_ref, between)
    out = dot(att_ref[...], proj_ref[...])
    x1_ref[...] = (x_ref[...].astype(F32) + norm(out, attn_gain_ref[...])).astype(BF16)
    pl.semaphore_wait(line_sem, len(across))

    def exchange(source, landing, send_sem, recv_sem, sign, group):
        def one(k, carry):
            rows = pl.ds(k * ROOM, ROOM)
            pltpu.make_async_remote_copy(
                src_ref=source.at[rows], dst_ref=landing.at[rows], send_sem=send_sem, recv_sem=recv_sem,
                device_id=(partner(k, sign), tall), device_id_type=MESH,
            ).start()
            return carry

        lax.fori_loop(max(1, group * per), group * per + per, one, 0)

    def whole_of(ref, blocks, send_sem, recv_sem):
        rows = pl.ds(0, blocks * ROOM)
        return pltpu.make_async_remote_copy(
            src_ref=ref.at[rows], dst_ref=ref.at[rows], send_sem=send_sem, recv_sem=recv_sem,
            device_id=(wide, down), device_id_type=MESH,
        )

    for pair in range(groups // 2):
        rows = slice(pair * span, pair * span + span)
        slots[rows] = dot(scatter[rows, :], x1_ref[...]).astype(BF16).reshape(span, WAYS, LANES)
        for group in (2 * pair, 2 * pair + 1):
            exchange(slots, arrived, give_send.at[0], give_recv.at[group], 1, group)
        if pair > 0:
            for kind, way, step in (((1, 0, 2),), ((0, 1, 2), (2, 0, 1)), ((1, 1, 2), (2, 1, 1)))[pair - 1]:
                onward(kind, way, step)
    arrived[0:ROOM] = slots[0:ROOM]
    logit = jnp.sum(dot(x1_ref[...], router_ref[...], NT) * chosen, axis=-1, keepdims=True)
    gate[...] = jnp.broadcast_to(in_use * jax.nn.sigmoid(logit), gate.shape)
    onward(0, 0, 3)
    onward(1, 0, 3)
    onward(2, 0, 2)
    hops[0, 1, 3].wait_recv()
    onward(1, 1, 3)
    onward(2, 1, 2)
    hops[0, 0, last].wait_recv()

    def finish(half, group):
        rows = slice(group * room, group * room + room)
        out = dot(hidden[group], w_out[half].reshape(n_tall * TILE, TILE)).astype(BF16)
        made[half, rows] = out.reshape(room, WAYS // 2, LANES)
        exchange(made.at[half], back.at[half], take_send.at[half], take_recv.at[half, group], -1, group)

    for group in range(groups):
        rows = slice(group * room, group * room + room)
        whole_of(arrived, per - (group == 0), give_send.at[0], give_recv.at[group]).wait_recv()
        here = arrived[rows].reshape(room, D)
        for c in range(n_tall):
            hidden[group, :, c * TILE : c * TILE + TILE] = gelu(dot(here, w_in[c])).astype(BF16)
        if group == 0:
            hops[1, 0, last].wait_recv()
            hops[1, 1, last].wait_recv()
        finish(0, group)
        if group < 2:
            onward(2, group, 3)
    hops[2, 0, last].wait_recv()
    hops[2, 1, last].wait_recv()
    for group in range(groups):
        finish(1, group)
    back[:, 0:ROOM] = made[:, 0:ROOM]
    for copy in hops.values():
        copy.wait_send()
    whole_of(slots, n_wide - 1, give_send.at[0], give_recv.at[0]).wait_send()
    for half in range(2):
        cols = slice(half * TILE, half * TILE + TILE)
        for pair in range(groups // 2):
            for group in (2 * pair, 2 * pair + 1):
                whole_of(
                    back.at[half], per - (group == 0), take_send.at[half], take_recv.at[half, group]
                ).wait_recv()
            part = dot(gather[pair], back[half, pair * span : pair * span + span].reshape(span, TILE))
            picked[:, cols] = part if pair == 0 else picked[:, cols] + part
    result_ref[...] = (
        x1_ref[...].astype(F32) + gate[:, 0:1] * norm(picked[...], moe_gain_ref[...])
    ).astype(BF16)
    for half in range(2):
        whole_of(made.at[half], n_wide - 1, take_send.at[half], take_recv.at[half, 0]).wait_send()


def body(
    tokens, qkv_weight, proj_weight, head_scale, attn_gain, router, expert_in, expert_out, moe_gain, expert_ids, keep
):
    n_tall, n_wide = lax.axis_size("tall"), lax.axis_size("wide")
    experts = router.shape[1]
    limits = (EDGE * n_tall, EDGE * n_wide)
    hidden = expert_in.shape[2]
    rows = pltpu.VMEM((TOK, D), BF16)
    slot_buffer = pltpu.VMEM((experts * ROOM, WAYS, LANES), BF16)
    half_buffer = pltpu.VMEM((2, experts * ROOM, WAYS // 2, LANES), BF16)
    DMA = pltpu.SemaphoreType.DMA
    ring_sem = DMA((2, n_tall // 2))
    out = pl.pallas_call(
        functools.partial(block_kernel, limits, experts),
        out_shape=jax.ShapeDtypeStruct((TOK, D), BF16),
        in_specs=[HBM, HBM, HBM, VMEM, SMEM, VMEM, HBM, HBM, VMEM, VMEM, VMEM],
        out_specs=VMEM,
        scratch_shapes=[
            rows, rows, rows,
            pltpu.VMEM((D, 3 * D), BF16),
            pltpu.VMEM((D, D), BF16),
            pltpu.VMEM((HEADS // GROUP, TOK, TILE), BF16),
            pltpu.VMEM((HEADS // GROUP, SPAN, TILE), BF16),
            pltpu.VMEM((HEADS // GROUP, GROUP * THIRD, TILE), BF16),
            pltpu.VMEM((HEADS // GROUP, SPAN, TILE), BF16),
            rows, rows, rows,
            pltpu.VMEM((experts * ROOM, TOK), BF16),
            pltpu.VMEM((4, TOK, experts * ROOM // 4), BF16),
            slot_buffer, slot_buffer, half_buffer, half_buffer,
            pltpu.VMEM((8, experts * ROOM // 8, n_tall * hidden), BF16),
            pltpu.VMEM((TOK, 128), F32),
            pltpu.VMEM((TOK, D), F32),
            pltpu.VMEM((n_tall, D, hidden), BF16),
            pltpu.VMEM((2, n_tall, hidden, TILE), BF16),
            DMA((6,)), pltpu.SemaphoreType.REGULAR, DMA((3,)), DMA((3,)), ring_sem, ring_sem,
            DMA((2, 2, n_tall // 2)), DMA((2, 2, n_tall // 2)), DMA((1,)), DMA((8,)), DMA((2,)), DMA((2, 8)),
        ],
        compiler_params=pltpu.CompilerParams(collective_id=0, has_side_effects=True, vmem_limit_bytes=62 << 20),
        name="block",
    )(
        tokens.reshape(TOK, D), qkv_weight, proj_weight, attn_gain.reshape(1, D), head_scale, router.T, expert_in[0],
        expert_out[0], moe_gain.reshape(1, D), expert_ids.reshape(1, TOK), keep.reshape(1, TOK),
    )
    return out.reshape(EDGE, EDGE, D)


def solution(mesh):
    placed = (
        P("tall", "wide", None), P(), P(), P(), P(), P(), P("wide", None, "tall"), P("wide", "tall", None), P(),
        P("tall", "wide", None, None), P("tall", "wide", None),
    )
    return jax.shard_map(
        body, mesh=mesh, in_specs=placed, out_specs=P("tall", "wide", None), check_vma=False
    )
```

```python
import functools
import math

import jax
import jax.numpy as jnp
from jax import lax
from jax.experimental import pallas as pl
from jax.experimental.pallas import tpu as pltpu
from jax.sharding import PartitionSpec as P

F32, BF16, I32 = jnp.float32, jnp.bfloat16, jnp.int32
MESH = pl.DeviceIdType.MESH
EDGE = 24
HALF = EDGE // 2
TOK = EDGE * EDGE
QUAD = HALF * HALF
HEADS = 16
HEAD = 32
D = 512
GROUP = 4
SPAN = GROUP * TOK
TILE = 256
LOG2E = math.log2(math.e)
ROOM = 13
LANES = 128
TRIPLE = 3
THIRD = TOK // TRIPLE
WAYS = D // LANES
NT = (((1,), (1,)), ((), ()))
TN = (((0,), (0,)), ((), ()))
VMEM = pl.BlockSpec(memory_space=pltpu.VMEM)
SMEM = pl.BlockSpec(memory_space=pltpu.SMEM)
HBM = pl.BlockSpec(memory_space=pltpu.HBM)


def dot(a, b, dims=None):
    if dims is None:
        return jnp.dot(a, b, preferred_element_type=F32)
    return lax.dot_general(a, b, dims, preferred_element_type=F32)


def iota(shape, axis):
    return lax.broadcasted_iota(I32, shape, axis)


def norm(value, gain):
    mean = jnp.mean(value, axis=-1, keepdims=True)
    centred = value - mean
    return centred * lax.rsqrt(jnp.mean(centred * centred, axis=-1, keepdims=True) + 1e-5) * gain


def gelu(value):
    return 0.5 * value * (1.0 + lax.erf(value * math.sqrt(0.5)))


def unit(block):
    ones = (iota((TILE, TILE), 0) // HEAD == iota((TILE, TILE), 1) // HEAD).astype(BF16)
    square = block * block
    high = square.astype(BF16)
    low = (square - high.astype(F32)).astype(BF16)
    return (block * lax.rsqrt(dot(high, ones) + dot(low, ones) + 1e-6)).astype(BF16)


def region_column(total_rows, total_cols, stride=1):
    place = iota((TOK // stride, 1), 0) * stride
    row = lax.axis_index("tall") * EDGE + place // EDGE
    col = lax.axis_index("wide") * EDGE + place % EDGE
    return (row + HALF >= total_rows).astype(I32) * 2 + (col + HALF >= total_cols).astype(I32)


def features(scale_ref, region, region3, q_ref, k_ref, k3_ref, v_ref):
    lane = iota((1, 128), 1)
    feat, own_head = lane % HEAD, lane // HEAD
    key_feat = jnp.where(feat < 12, jnp.where(region == feat % 4, 0.0, -1.0), jnp.where(feat == 12, 1.0, 0.0))
    key3_feat = jnp.where(jnp.logical_and(feat < 12, region3 != feat % 4), -1.0, 0.0)
    for g in range(HEADS // GROUP):
        scale = jnp.ones((1, 128), F32)
        for h in range(GROUP):
            scale = jnp.where(own_head == h, scale_ref[g * GROUP + h], scale)
        whole = 100.0 / scale
        high = whole.astype(BF16).astype(F32)
        middle = (whole - high).astype(BF16).astype(F32)
        piece = jnp.where(feat < 4, high, jnp.where(feat < 8, middle, whole - high - middle))
        query_feat = jnp.where(jnp.logical_and(feat < 12, region == feat % 4), piece, 0.0)
        q_ref[g, :, 128:256] = query_feat.astype(BF16)
        for h in range(GROUP):
            mine = own_head == h
            rows = slice(h * TOK, h * TOK + TOK)
            k_ref[g, rows, 128:256] = jnp.where(mine, key_feat, 0.0).astype(BF16)
            k3_ref[g, h * THIRD : h * THIRD + THIRD, 128:256] = jnp.where(mine, key3_feat, 0.0).astype(BF16)
            v_ref[g, rows, 128:256] = jnp.broadcast_to(jnp.where(mine, 1.0, 0.0), (TOK, 128)).astype(BF16)


def prepare(x, qkv_ref, q_ref, k_ref, k3_ref, v_ref):
    own_head = iota((1, 128), 1) // HEAD
    thirds = (iota((THIRD, TOK), 1) // TRIPLE == iota((THIRD, TOK), 0)).astype(BF16)
    for half in range(2):
        at = TILE * half
        qn = unit(dot(x, qkv_ref[:, at : at + TILE]))
        kn = unit(dot(x, qkv_ref[:, D + at : D + at + TILE]))
        k3 = (dot(thirds, kn) * (1.0 / TRIPLE)).astype(BF16)
        vb = dot(x, qkv_ref[:, 2 * D + at : 2 * D + at + TILE]).astype(BF16)
        for sub in range(2):
            g = 2 * half + sub
            cut = slice(128 * sub, 128 * sub + 128)
            q_ref[g, :, 0:128] = qn[:, cut]
            for h in range(GROUP):
                mine = own_head == h
                rows = slice(h * TOK, h * TOK + TOK)
                k_ref[g, rows, 0:128] = jnp.where(mine, kn[:, cut], jnp.zeros((), BF16))
                k3_ref[g, h * THIRD : h * THIRD + THIRD, 0:128] = jnp.where(mine, k3[:, cut], jnp.zeros((), BF16))
                v_ref[g, rows, 0:128] = jnp.where(mine, vb[:, cut], jnp.zeros((), BF16))


def lane_scales(scale_ref, g):
    out = jnp.zeros((1, SPAN), F32)
    for h in range(GROUP):
        out = jnp.where(iota((1, SPAN), 1) // TOK == h, scale_ref[g * GROUP + h] * LOG2E, out)
    return out


def attend(q_ref, k_ref, k3_ref, v_ref, scale_ref, att_ref, between):
    lane = iota((1, 128), 1)
    for g in range(HEADS // GROUP):
        shifted = q_ref[g, :, 128:256]
        score = dot(q_ref[g], k3_ref[g], NT)
        tops = [None] * GROUP
        for n in range(GROUP * THIRD // 128):
            piece = score[:, 128 * n : 128 * n + 128]
            low, high = 128 * n // THIRD, (128 * n + 127) // THIRD
            edge = high * THIRD - 128 * n
            for h in range(low, high + 1):
                part = piece
                if low != high:
                    part = jnp.where((lane < edge) if h == low else (lane >= edge), piece, -jnp.inf)
                tops[h] = part if tops[h] is None else jnp.maximum(tops[h], part)
        for h in range(GROUP):
            shift = -(jnp.max(tops[h], axis=-1, keepdims=True) + 2.0 / 3.0)
            shifted = jnp.where(lane == h * HEAD + 12, shift.astype(BF16), shifted)
        q_ref[g, :, 128:256] = shifted
        scales = lane_scales(scale_ref, g)
        acc = None
        for j in range(SPAN // TILE):
            at = slice(TILE * j, TILE * j + TILE)
            powers = jnp.exp2(dot(q_ref[g], k_ref[g, at, :], NT) * scales[:, at]).astype(BF16)
            part = dot(powers, v_ref[g, at, :])
            acc = part if acc is None else acc + part
        att_ref[:, 128 * g : 128 * g + 128] = (acc[:, :128] / acc[:, 128:]).astype(BF16)
        between(g)


def ring_hop(own, gathered, way, step, send_sem, recv_sem):
    tall, wide, n_tall = lax.axis_index("tall"), lax.axis_index("wide"), lax.axis_size("tall")
    owner = lax.rem(tall + n_tall + (1 - step if way == 0 else step - 1), n_tall)
    return pltpu.make_async_remote_copy(
        src_ref=own if step == 1 else gathered.at[owner],
        dst_ref=gathered.at[owner],
        send_sem=send_sem.at[way, step - 1],
        recv_sem=recv_sem.at[way, step - 1],
        device_id=(wide, lax.rem(tall + (1 if way == 0 else n_tall - 1), n_tall)),
        device_id_type=MESH,
    )


def rem(a, n):
    return lax.rem(a, jnp.int32(n))


def div(a, n):
    return lax.div(a, jnp.int32(n))


def partner(k, sign):
    wide = lax.axis_index("wide")
    core, x, y = rem(wide, 2), rem(div(wide, 2), 4), div(wide, 8)
    turn = rem(64 - k, 64)
    step = rem(turn, 8)
    size = div(step + 1, 2)
    dy = size + rem(step + 1, 2) * (8 - 2 * size)
    dx, dc = rem(div(turn, 8), 4), div(turn, 32)
    return (rem(y + 8 + sign * dy, 8) * 4 + rem(x + 4 + sign * dx, 4)) * 2 + rem(core + 2 + sign * dc, 2)


def place_of(expert):
    wide = lax.axis_index("wide")
    dc = (expert % 2 + 2 - wide % 2) % 2
    dx = (expert // 2 % 4 + 4 - wide // 2 % 4) % 4
    dy = (expert // 8 + 8 - wide // 8) % 8
    step = jnp.where(dy == 0, 0, jnp.where(dy <= 4, 2 * dy - 1, 16 - 2 * dy))
    return (64 - (dc * 32 + dx * 8 + step)) % 64


def block_kernel(
    limits, experts,
    tokens_hbm, qkv_hbm, proj_hbm, attn_gain_ref, scale_ref, router_ref, in_hbm, out_hbm, moe_gain_ref, ids_ref, keep_ref,
    result_ref,
    tokens_ref, send, recv, qkv_ref, proj_ref, q_ref, k_ref, k3_ref, v_ref, att_ref, x_ref, x1_ref,
    scatter, gather, slots, arrived, made, back, hidden, gate, picked, w_in, w_out,
    load_sem, line_sem, send_sem, recv_sem, in_send, in_recv, out_send, out_recv, give_send, give_recv, take_send, take_recv,
):
    tall, wide = lax.axis_index("tall"), lax.axis_index("wide")
    n_tall, n_wide = lax.axis_size("tall"), lax.axis_size("wide")
    last = n_tall // 2
    loads = [
        pltpu.make_async_copy(tokens_hbm, tokens_ref, load_sem.at[0]),
        pltpu.make_async_copy(qkv_hbm, qkv_ref, load_sem.at[1]),
        pltpu.make_async_copy(proj_hbm, proj_ref, load_sem.at[2]),
        pltpu.make_async_copy(in_hbm, w_in.at[tall], load_sem.at[3]),
        pltpu.make_async_copy(out_hbm, w_out.at[tall], load_sem.at[4]),
    ]
    for load in loads:
        load.start()

    up, left = lax.rem(tall + n_tall - 1, n_tall), lax.rem(wide + n_wide - 1, n_wide)
    down, right = lax.rem(tall + 1, n_tall), lax.rem(wide + 1, n_wide)
    barrier = pltpu.get_barrier_semaphore()
    near = [(wide, up), (wide, down), (left, up), (right, down), (left, tall), (right, tall)]
    row_start, row_place = div(wide, 8) * 8, rem(wide, 8)
    across = [(rem(wide + 8 * i, n_wide), tall) for i in range(1, 8)]
    near += across + [(row_start + rem(row_place + i, 8), tall) for i in range(1, 8)]
    for peer in near:
        pl.semaphore_signal(barrier, inc=1, device_id=peer, device_id_type=MESH)

    place = iota((TOK, TOK), 0)
    quad, rest = place // QUAD, place % QUAD
    row = rest // HALF + jnp.where(quad % 2 == 0, HALF, 0)
    col = rest % HALF + jnp.where(quad < 2, HALF, 0)
    pick = (iota((TOK, TOK), 1) == row * EDGE + col).astype(BF16)
    loads[0].wait()
    send[...] = dot(pick, tokens_ref[...]).astype(BF16)
    recv[0:QUAD, :] = send[0:QUAD, :]
    pl.semaphore_wait(barrier, len(near))
    copies = []
    for i, peer in enumerate([(wide, up), (left, tall), (left, up)]):
        rows = pl.ds(QUAD * (i + 1), QUAD)
        copies.append(
            pltpu.make_async_remote_copy(
                src_ref=send.at[rows], dst_ref=recv.at[rows], send_sem=send_sem.at[i], recv_sem=recv_sem.at[i],
                device_id=peer, device_id_type=MESH,
            )
        )
        copies[-1].start()

    hops = {}

    def launch(kind, way, step):
        if step < last or (kind == 0 and way == 0):
            if kind == 0:
                copy = ring_hop(in_hbm, w_in, way, step, in_send, in_recv)
            else:
                copy = ring_hop(out_hbm, w_out, way, step, out_send, out_recv)
        else:
            owner = lax.rem(tall + (n_tall + 1 - last if way == 0 else last - 1), n_tall)
            rows = pl.ds(TILE // 2 * way, TILE // 2)
            copy = pltpu.make_async_remote_copy(
                src_ref=w_out.at[owner, rows], dst_ref=w_out.at[owner, rows], send_sem=out_send.at[way, last - 1],
                recv_sem=out_recv.at[way, last - 1], device_id=(wide, down if way == 0 else up), device_id_type=MESH,
            )
        copy.start()
        hops[kind, way, step] = copy

    def onward(kind, way, step):
        hops[kind, way, step].wait_recv()
        launch(kind, way, step + 1)

    launch(0, 0, 1)
    for peer in across:
        pl.semaphore_signal(line_sem, inc=1, device_id=peer, device_id_type=MESH)

    per = 8
    groups = n_wide // per
    room = per * ROOM
    span = 2 * room
    ids, kept = ids_ref[...], keep_ref[...] == 1
    named = iota((experts, TOK), 0) == ids
    live = jnp.where(jnp.logical_and(named, kept), 1.0, 0.0)
    earlier = (iota((TOK, TOK), 0) < iota((TOK, TOK), 1)).astype(BF16)
    slot = jnp.sum(jnp.where(named, dot(live.astype(BF16), earlier), 0.0), axis=0, keepdims=True)
    target = jnp.where(kept, place_of(ids) * ROOM + slot.astype(I32), -1)
    scatter[...] = (iota((experts * ROOM, TOK), 0) == target).astype(BF16)
    eye = (iota((experts, experts), 0) == iota((experts, experts), 1)).astype(BF16)
    chosen = dot(live.astype(BF16), eye, TN)
    slot = jnp.sum(dot((live * slot).astype(BF16), eye, TN), axis=-1, keepdims=True)
    block = jnp.sum(chosen * place_of(iota((1, experts), 1)).astype(F32), axis=-1, keepdims=True)
    in_use = jnp.sum(chosen, axis=-1, keepdims=True)
    landing = jnp.where(in_use > 0.5, block * ROOM + slot, -1.0).astype(I32)
    for pair in range(groups // 2):
        gather[pair] = (iota((TOK, span), 1) + pair * span == landing).astype(BF16)

    launch(1, 0, 1)
    features(scale_ref, region_column(*limits), region_column(*limits, TRIPLE), q_ref, k_ref, k3_ref, v_ref)
    row, col = place // EDGE, place % EDGE
    quad = (row // HALF) + 2 * (col // HALF)
    pick = (iota((TOK, TOK), 1) == quad * QUAD + (row % HALF) * HALF + col % HALF).astype(BF16)
    for load in loads[1:]:
        load.wait()
    for copy in copies:
        copy.wait()
    launch(0, 1, 1)
    x = dot(pick, recv[...]).astype(BF16)
    x_ref[...] = x
    prepare(x, qkv_ref, q_ref, k_ref, k3_ref, v_ref)
    launch(1, 1, 1)

    def between(g):
        for kind, way, step in (((0, 0, 1),), ((1, 0, 1),), (), ((0, 1, 1),))[g]:
            onward(kind, way, step)

    attend(q_ref, k_ref, k3_ref, v_ref, scale_ref, att_ref, between)
    out = dot(att_ref[...], proj_ref[...])
    x1_ref[...] = (x_ref[...].astype(F32) + norm(out, attn_gain_ref[...])).astype(BF16)
    pl.semaphore_wait(line_sem, len(across))

    def exchange(source, landing, send_sem, recv_sem, sign, group):
        def one(k, carry):
            rows = pl.ds(k * ROOM, ROOM)
            pltpu.make_async_remote_copy(
                src_ref=source.at[rows], dst_ref=landing.at[rows], send_sem=send_sem, recv_sem=recv_sem.at[group],
                device_id=(partner(k, sign), tall), device_id_type=MESH,
            ).start()
            return carry

        lax.fori_loop(max(1, group * per), group * per + per, one, 0)

    def whole_of(ref, blocks, send_sem, recv_sem):
        rows = pl.ds(0, blocks * ROOM)
        return pltpu.make_async_remote_copy(
            src_ref=ref.at[rows], dst_ref=ref.at[rows], send_sem=send_sem, recv_sem=recv_sem,
            device_id=(wide, down), device_id_type=MESH,
        )

    for pair in range(groups // 2):
        rows = slice(pair * span, pair * span + span)
        slots[rows] = dot(scatter[rows, :], x1_ref[...]).astype(BF16).reshape(span, WAYS, LANES)
        for group in (2 * pair, 2 * pair + 1):
            exchange(slots, arrived, give_send.at[0], give_recv, 1, group)
        if pair % 2 == 0:
            onward(*((1, 1, 1), (0, 0, 2))[pair // 2])
    arrived[0:ROOM] = slots[0:ROOM]
    for kind, way, step in ((1, 0, 2), (0, 1, 2), (1, 1, 2)):
        onward(kind, way, step)
    logit = jnp.sum(dot(x1_ref[...], router_ref[...], NT) * chosen, axis=-1, keepdims=True)
    gate[...] = jnp.broadcast_to(in_use * jax.nn.sigmoid(logit), gate.shape)
    onward(0, 0, 3)
    onward(1, 0, 3)
    hops[0, 1, 3].wait_recv()
    onward(1, 1, 3)
    hops[0, 0, last].wait_recv()
    for group in range(groups):
        rows = slice(group * room, group * room + room)
        whole_of(arrived, per - (group == 0), give_send.at[0], give_recv.at[group]).wait_recv()
        here = arrived[rows].reshape(room, D)
        for c in range(n_tall):
            hidden[:, c * TILE : c * TILE + TILE] = gelu(dot(here, w_in[c])).astype(BF16)
        if group == 0:
            hops[1, 0, last].wait_recv()
            hops[1, 1, last].wait_recv()
        out = dot(hidden[...], w_out[...].reshape(n_tall * TILE, D)).astype(BF16)
        made[rows] = out.reshape(room, WAYS, LANES)
        exchange(made, back, take_send.at[0], take_recv, -1, group)
    back[0:ROOM] = made[0:ROOM]
    for copy in hops.values():
        copy.wait_send()
    whole_of(slots, n_wide - 1, give_send.at[0], give_recv.at[0]).wait_send()
    for pair in range(groups // 2):
        for group in (2 * pair, 2 * pair + 1):
            whole_of(back, per - (group == 0), take_send.at[0], take_recv.at[group]).wait_recv()
        part = dot(gather[pair], back[pair * span : pair * span + span].reshape(span, D))
        if pair < groups // 2 - 1:
            picked[...] = part if pair == 0 else picked[...] + part
    result_ref[...] = (
        x1_ref[...].astype(F32) + gate[:, 0:1] * norm(picked[...] + part, moe_gain_ref[...])
    ).astype(BF16)
    whole_of(made, n_wide - 1, take_send.at[0], take_recv.at[0]).wait_send()


def body(
    tokens, qkv_weight, proj_weight, head_scale, attn_gain, router, expert_in, expert_out, moe_gain, expert_ids, keep
):
    n_tall, n_wide = lax.axis_size("tall"), lax.axis_size("wide")
    experts = router.shape[1]
    limits = (EDGE * n_tall, EDGE * n_wide)
    hidden = expert_in.shape[2]
    rows = pltpu.VMEM((TOK, D), BF16)
    slot_buffer = pltpu.VMEM((experts * ROOM, WAYS, LANES), BF16)
    DMA = pltpu.SemaphoreType.DMA
    ring_sem = DMA((2, n_tall // 2))
    out = pl.pallas_call(
        functools.partial(block_kernel, limits, experts),
        out_shape=jax.ShapeDtypeStruct((TOK, D), BF16),
        in_specs=[HBM, HBM, HBM, VMEM, SMEM, VMEM, HBM, HBM, VMEM, VMEM, VMEM],
        out_specs=VMEM,
        scratch_shapes=[
            rows, rows, rows,
            pltpu.VMEM((D, 3 * D), BF16),
            pltpu.VMEM((D, D), BF16),
            pltpu.VMEM((HEADS // GROUP, TOK, TILE), BF16),
            pltpu.VMEM((HEADS // GROUP, SPAN, TILE), BF16),
            pltpu.VMEM((HEADS // GROUP, GROUP * THIRD, TILE), BF16),
            pltpu.VMEM((HEADS // GROUP, SPAN, TILE), BF16),
            rows, rows, rows,
            pltpu.VMEM((experts * ROOM, TOK), BF16),
            pltpu.VMEM((4, TOK, experts * ROOM // 4), BF16),
            slot_buffer, slot_buffer, slot_buffer, slot_buffer,
            pltpu.VMEM((experts * ROOM // 8, n_tall * hidden), BF16),
            pltpu.VMEM((TOK, 128), F32),
            pltpu.VMEM((TOK, D), F32),
            pltpu.VMEM((n_tall, D, hidden), BF16),
            pltpu.VMEM((n_tall, hidden, D), BF16),
            DMA((5,)), pltpu.SemaphoreType.REGULAR, DMA((3,)), DMA((3,)), ring_sem, ring_sem, ring_sem, ring_sem,
            DMA((1,)), DMA((8,)), DMA((1,)), DMA((8,)),
        ],
        compiler_params=pltpu.CompilerParams(collective_id=0, has_side_effects=True, vmem_limit_bytes=62 << 20),
        name="block",
    )(
        tokens.reshape(TOK, D), qkv_weight, proj_weight, attn_gain.reshape(1, D), head_scale, router.T, expert_in[0],
        expert_out[0], moe_gain.reshape(1, D), expert_ids.reshape(1, TOK), keep.reshape(1, TOK),
    )
    return out.reshape(EDGE, EDGE, D)


def solution(mesh):
    placed = (
        P("tall", "wide", None), P(), P(), P(), P(), P(), P("wide", None, "tall"), P("wide", "tall", None), P(),
        P("tall", "wide", None, None), P("tall", "wide", None),
    )
    return jax.shard_map(
        body, mesh=mesh, in_specs=placed, out_specs=P("tall", "wide", None), check_vma=False
    )
```
